128 devices in a mesh: batch: 16 (over y, z), head: 8 (over x, core).
Axes of the slice: x: 4, y: 4, z: 4, core: 2. Of those that a mesh axis runs over, the one named last changes fastest.
Arguments:
- hidden_in: bfloat16 [1024, 3, 2048], P(('batch', 'head')), may hold values from -6 to 6
- states: float32 [1024, 16, 128, 128], P('batch', 'head'), may hold values from -0.8 to 0.8
- norm_in: float32 [2048], replicated, may hold values from 0.1 to 1.9
- w_qk: bfloat16 [2048, 8, 2, 128], P(None, 'head'), may hold values from -0.125 to 0.125
- w_vz: bfloat16 [2048, 16, 2, 128], P(None, 'head'), may hold values from -0.125 to 0.125
- w_ba: bfloat16 [2048, 2, 16], P(None, None, 'head'), may hold values from -0.125 to 0.125
- a_log: float32 [16], P('head'), may hold values from -4 to 1.5
- dt_bias: float32 [16], P('head'), may hold values from -2 to 1
- norm_gate: float32 [128], replicated, may hold values from 0.1 to 1.9
- w_out: bfloat16 [16, 128, 2048], P('head'), may hold values from -0.125 to 0.125
- norm_post: float32 [2048], replicated, may hold values from 0.1 to 1.9
- shared_in: bfloat16 [2048, 2, 512], P('head'), may hold values from -0.125 to 0.125
- shared_gate: bfloat16 [2048], P('head'), may hold values from -0.125 to 0.125
- shared_out: bfloat16 [512, 2048], P(None, 'head'), may hold values from -0.25 to 0.25
- expert_in: bfloat16 [256, 2048, 2, 512], P(('batch', 'head')), may hold values from -0.125 to 0.125
- expert_out: bfloat16 [256, 512, 2048], P(('batch', 'head')), may hold values from -0.25 to 0.25
- routes: int32 [1024, 3, 10], P(('batch', 'head')), may hold values from 0 to 255, all different within a row; in each aligned block of 24 rows (0 to 23, 24 to 47, ..., all dimensions but the last counted through in order) at most 2 rows name the same one
- route_weight: float32 [1024, 3, 10], P(('batch', 'head')), may hold values from 0.02 to 0.25
Outputs:
- layer_out: bfloat16 [1024, 3, 2048], P('batch', None, 'head')
The draws below stay inside these ranges and needn't reach their ends.
Inputs may be any that keep to these rules, and one draw needn't show every extreme that they name: `routes`: among the 240 choices of one device's tokens, no expert is named more than 2 times, a bound that some block reaches; a token's 10 experts differ.
All inputs are finite; a program needn't handle non-finite values.
Results may differ from the reference program's by a relative error of at most 0.009.
Values may be sent and summed in bfloat16 or wider, within the bound.
A program may use at most 128 MiB of HBM per device.

```python
import math
import jax
import jax.numpy as jnp
import numpy as np
from jax import lax

D = 2048
HK = 8
HV = 16
DK = 128
DV = 128
FFE = 512
FFS = 512
TOPK = 10
STEPS = 3
SEQ_DEV = 8
SEQS = 1024
EXPERTS = 256
CAP = 2
N_BATCH = 16
N_HEAD = 8


def block_levels(stream_key, shape, shards, smallest, high):
    def one(position, blocks):
        steps = jax.random.uniform(jax.random.fold_in(jax.random.fold_in(stream_key, 6), position), (blocks,), jnp.float32, smallest / len(shards), high / len(shards))
        return jnp.repeat(jnp.exp(steps), shape[position] // blocks).reshape((-1,) + (1,) * (len(shape) - position - 1))

    loudness = one(*shards[0])
    for cut in shards[1:]:
        loudness = loudness * one(*cut)
    return loudness


def assign_block(key, own, number, rows, amount, top, reach, lean):
    sequence = jax.random.permutation(key, amount)
    heavy_load, common = portions_of(amount, rows * top, reach, lean, True), portions_of(amount, rows * top, reach, lean, False)
    places = jnp.arange(amount)

    def named(sizes, turn):
        used = int((sizes > 0).sum())
        fixed = max(1, used // 4)
        shifted = fixed + (places - fixed + turn * (used - fixed)) % max(1, amount - fixed)
        return jnp.zeros((amount,), jnp.int32).at[sequence[jnp.where(places < fixed, places, shifted)]].set(jnp.asarray(sizes, jnp.int32))

    sizes = jnp.where(number % 4 == 0, named(heavy_load, number // 4), named(common, number - number // 4 - 1))
    mixed = jax.random.permutation(jax.random.fold_in(own, 3), amount)
    source_of, sink = mixed[0:amount // 2 * 2:2], mixed[1:amount // 2 * 2:2]
    room = jnp.minimum(sizes[source_of] - 1, reach - sizes[sink]) // 2
    room = jnp.where((source_of == sequence[0]) | (sink == sequence[0]) | (sizes[sink] == 0), 0, jnp.maximum(room, 0))
    shifted = jax.random.randint(jax.random.fold_in(own, 4), (amount // 2,), 0, 1 << 20) % (room + 1)
    sizes = sizes.at[source_of].add(-shifted).at[sink].add(shifted)
    members = jnp.searchsorted(jnp.cumsum(sizes), jnp.arange(rows * top), side="right").astype(jnp.int32)
    grid = members.reshape(top, rows).T
    grid = grid[jax.random.permutation(jax.random.fold_in(own, 1), rows)]
    turn = jax.random.randint(jax.random.fold_in(own, 2), (rows, 1), 0, top)
    return jnp.take_along_axis(grid, (jnp.arange(top)[None, :] + turn) % top, axis=1)


def portions_of(amount, total, bound, slope, full):
    portions = [(1 << 20) // math.isqrt(grade ** slope) + 1 for grade in range(1, amount + 1)]
    largest = bound if full else min(bound, max(-(-total // amount), total * portions[0] // sum(portions)))
    least = 1 if total - largest >= amount - 1 else 0
    given, spare = [largest] + [least] * (amount - 1), total - largest - least * (amount - 1)
    while spare > 0:
        candidates = [i for i in range(1, amount) if given[i] < largest] or [i for i in range(1, amount) if given[i] < bound]
        whole, left = sum([portions[i] for i in candidates]), spare
        for i in candidates:
            more = min(bound - given[i], max(1, left * portions[i] // whole), spare)
            given[i] = given[i] + more
            spare = spare - more
    return np.array(given)


def normal_values(own_key, shape, deviation, most, split=(), kind=jnp.bfloat16):
    result = jax.random.normal(own_key, shape, jnp.float32) * deviation
    if len(split) > 0:
        result = block_levels(own_key, shape, split, -0.22, 0.18) * result
    return jnp.clip(result, min=-most, max=most).astype(kind)


def setup_inputs(seed: int = 0) -> dict:
    splits = jax.random.split(jax.random.key(seed), 19)
    hidden_in = normal_values(splits[0], (SEQS, STEPS, D), 1.0, 6.0, ((0, 128),))
    states = normal_values(splits[1], (SEQS, HV, DK, DV), 0.1, 0.8, ((0, 16), (1, 8)), jnp.float32)
    norm_in = jnp.clip(1.0 + 0.18 * jax.random.normal(splits[2], (D,), jnp.float32), 0.1, 1.9)
    w_qk = normal_values(splits[3], (D, HK, 2, DK), D ** -0.5, 0.125, ((1, 8),))
    w_vz = normal_values(splits[4], (D, HV, 2, DV), D ** -0.5, 0.125, ((1, 8),))
    w_ba = normal_values(splits[5], (D, 2, HV), D ** -0.5, 0.125, ((2, 8),))
    a_log = jnp.clip(-4.0 + 5.5 * jax.random.uniform(splits[6], (HV,), jnp.float32) ** block_levels(splits[6], (HV,), ((0, 8),), -0.2, 0.2), -4.0, 1.5)
    dt_bias = jnp.clip(-2.0 + 3.0 * jax.random.uniform(splits[7], (HV,), jnp.float32) ** block_levels(splits[7], (HV,), ((0, 8),), -0.2, 0.2), -2.0, 1.0)
    norm_gate = jnp.clip(1.0 + 0.18 * jax.random.normal(splits[8], (DV,), jnp.float32), 0.1, 1.9)
    w_out = normal_values(splits[9], (HV, DV, D), (HV * DV) ** -0.5, 0.125, ((0, 8),))
    norm_post = jnp.clip(1.0 + 0.18 * jax.random.normal(splits[10], (D,), jnp.float32), 0.1, 1.9)
    shared_in = normal_values(splits[11], (D, 2, FFS), D ** -0.5, 0.125, ((0, 8),))
    shared_gate = normal_values(splits[12], (D,), D ** -0.5, 0.125, ((0, 8),))
    shared_out = normal_values(splits[13], (FFS, D), FFS ** -0.5, 0.25, ((1, 8),))
    expert_in = normal_values(splits[14], (EXPERTS, D, 2, FFE), D ** -0.5, 0.125, ((0, 128),))
    expert_out = normal_values(splits[15], (EXPERTS, FFE, D), FFE ** -0.5, 0.25, ((0, 128),))
    routes_keys = jax.random.split(jax.random.fold_in(splits[16], 1), SEQS * STEPS // (SEQ_DEV * STEPS))
    routes_turns = jax.random.permutation(jax.random.fold_in(splits[16], 3), SEQS * STEPS // (SEQ_DEV * STEPS))
    routes = jax.vmap(lambda own, number: assign_block(jax.random.fold_in(splits[16], 2), own, number, SEQ_DEV * STEPS, EXPERTS, TOPK, CAP, 2))(routes_keys, routes_turns).reshape((SEQS, STEPS, TOPK))
    route_weight = jnp.clip(jnp.exp(math.log(0.25) - 2.5257287 * jax.random.uniform(splits[17], (SEQS, STEPS, TOPK), jnp.float32) ** block_levels(splits[17], (SEQS, STEPS, TOPK), ((0, 128),), -0.2, 0.2)), 0.02, 0.25)
    return {"hidden_in": hidden_in, "states": states, "norm_in": norm_in, "w_qk": w_qk, "w_vz": w_vz, "w_ba": w_ba, "a_log": a_log, "dt_bias": dt_bias, "norm_gate": norm_gate, "w_out": w_out, "norm_post": norm_post, "shared_in": shared_in, "shared_gate": shared_gate, "shared_out": shared_out, "expert_in": expert_in, "expert_out": expert_out, "routes": routes, "route_weight": route_weight}


EPS = 1e-06

def rms_scale(values, gain):
    return values * lax.rsqrt(lax.optimization_barrier(jnp.mean(values * values, axis=-1, keepdims=True)) + EPS) * gain

def unit_norm(values):
    return values * lax.rsqrt(lax.optimization_barrier(jnp.sum(values * values, axis=-1, keepdims=True)) + EPS)

def reference(hidden_in, states, norm_in, w_qk, w_vz, w_ba, a_log, dt_bias, norm_gate, w_out, norm_post, shared_in, shared_gate, shared_out, expert_in, expert_out, routes, route_weight):
    f32 = jnp.float32
    bf16 = jnp.bfloat16
    highest = lax.Precision.HIGHEST
    normed = rms_scale(hidden_in.astype(f32), norm_in).astype(bf16)
    proj_qk = jnp.einsum('std,dhck->sthck', normed.astype(f32), w_qk.astype(f32))
    proj_vz = jnp.einsum('std,dhcv->sthcv', normed.astype(f32), w_vz.astype(f32))
    proj_ba = jnp.einsum('std,dch->stch', normed.astype(f32), w_ba.astype(f32))
    ratio = HV // HK
    query = jnp.repeat(unit_norm(jax.nn.silu(proj_qk[:, :, :, 0, :])) * DK ** (-0.5), ratio, axis=2)
    keys = jnp.repeat(unit_norm(jax.nn.silu(proj_qk[:, :, :, 1, :])), ratio, axis=2)
    values = jax.nn.silu(proj_vz[:, :, :, 0, :])
    gate_z = proj_vz[:, :, :, 1, :]
    beta = jax.nn.sigmoid(proj_ba[:, :, 0, :])
    decay = jnp.exp(-jnp.exp(a_log) * jax.nn.softplus(proj_ba[:, :, 1, :] + dt_bias))
    memory = states
    readouts = []
    for step in range(STEPS):
        memory = memory * decay[:, step, :, None, None]
        recalled = jnp.einsum('shkv,shk->shv', memory, keys[:, step], precision=highest)
        delta = beta[:, step, :, None] * (values[:, step] - recalled)
        memory = memory + keys[:, step, :, :, None] * delta[:, :, None, :]
        readouts.append(jnp.einsum('shkv,shk->shv', memory, query[:, step], precision=highest))
    readout = jnp.stack(readouts, axis=1)
    gated = (rms_scale(readout, norm_gate) * jax.nn.silu(gate_z)).astype(bf16)
    attn = jnp.einsum('sthv,hvd->std', gated.astype(f32), w_out.astype(f32))
    resid = (hidden_in.astype(f32) + attn).astype(bf16)
    post = rms_scale(resid.astype(f32), norm_post).astype(bf16)
    gate_up = jnp.einsum('std,dcf->stcf', post.astype(f32), shared_in.astype(f32))
    logit = jnp.einsum('std,d->st', post.astype(f32), shared_gate.astype(f32))
    shared_mid = (jax.nn.silu(gate_up[:, :, 0, :]) * gate_up[:, :, 1, :]).astype(bf16)
    shared_y = jnp.einsum('stf,fd->std', shared_mid.astype(f32), shared_out.astype(f32)) * jax.nn.sigmoid(logit)[:, :, None]
    devices = N_BATCH * N_HEAD
    token_count = SEQS * STEPS
    block = SEQ_DEV * STEPS * TOPK
    flat_ids = routes.reshape(devices, block)
    hot = (flat_ids[:, :, None] == jnp.arange(EXPERTS, dtype=jnp.int32)[None, None, :]).astype(jnp.int32)
    ranks = lax.optimization_barrier(jnp.sum((jnp.cumsum(hot, axis=1) - 1) * hot, axis=2))
    source = jnp.arange(devices, dtype=jnp.int32)[:, None] * CAP
    columns = (source + ranks).reshape(-1)
    ids = flat_ids.reshape(-1)
    token_of = jnp.arange(token_count * TOPK, dtype=jnp.int32) // TOPK
    table = jnp.full((EXPERTS, devices * CAP), token_count, jnp.int32).at[ids, columns].set(token_of)
    rows_all = jnp.concatenate([post.reshape(token_count, D), jnp.zeros((1, D), bf16)], axis=0)

    def one_expert(pieces):
        index, weights_in, weights_out = pieces
        rows = rows_all[index]
        mixed = jnp.dot(rows, weights_in.reshape(D, 2 * FFE), preferred_element_type=f32)
        inner = (jax.nn.silu(mixed[:, :FFE]) * mixed[:, FFE:]).astype(bf16)
        return jnp.dot(inner, weights_out, preferred_element_type=f32).astype(bf16)
    expert_y = lax.map(one_expert, (table, expert_in, expert_out))
    picked = expert_y[ids, columns].astype(f32).reshape(token_count, TOPK, D)
    routed = lax.optimization_barrier(jnp.sum(route_weight.reshape(token_count, TOPK, 1) * picked, axis=1)).astype(bf16)
    routed = routed.reshape(SEQS, STEPS, D)
    return (resid.astype(f32) + shared_y + routed.astype(f32)).astype(bf16)
```

```python
import functools

import jax
import jax.numpy as jnp
from jax import lax
from jax.experimental import pallas as pl
from jax.experimental.pallas import tpu as pltpu
from jax.sharding import PartitionSpec as P

EPS = 1e-06
MESH = pl.DeviceIdType.MESH
HEADS = 8
BATCH = 16
DEVS = HEADS * BATCH
F32 = jnp.float32
BF16 = jnp.bfloat16
VMEM = pl.BlockSpec(memory_space=pltpu.VMEM)


def rms_scale(values, gain):
    return values * lax.rsqrt(jnp.mean(values * values, axis=-1, keepdims=True) + EPS) * gain


def silu(v):
    return v * jax.nn.sigmoid(v)


def spot(p):
    return (p // HEADS, p % HEADS)


def gather_kernel(own_ref, all_ref, send_sem, recv_sem, local_sem):
    b = lax.axis_index("batch")
    h = lax.axis_index("head")
    x, c = h // 2, h % 2
    sib = x * 2 + 1 - c
    chips = [(x + d) % 4 for d in (1, 3, 2)]
    barrier = pltpu.get_barrier_semaphore()
    for to in [sib] + [v * 2 + c for v in chips]:
        pl.semaphore_signal(barrier, inc=1, device_id=(b, to), device_id_type=MESH)
    pl.semaphore_wait(barrier, 4)
    mine = pltpu.make_async_copy(own_ref, all_ref.at[:, h], local_sem)
    mine.start()
    sent = []

    def send(src, slot, to):
        copy = pltpu.make_async_remote_copy(
            src_ref=src,
            dst_ref=all_ref.at[:, slot],
            send_sem=send_sem.at[len(sent)],
            recv_sem=recv_sem.at[slot],
            device_id=(b, to),
            device_id_type=MESH,
        )
        copy.start()
        sent.append(copy)

    def arrived(slot):
        pltpu.make_async_copy(own_ref, all_ref.at[:, slot], recv_sem.at[slot]).wait()

    for v in chips:
        send(own_ref, h, v * 2 + c)
    send(own_ref, h, sib)
    for d in (3, 1, 2):
        slot = ((x + d) % 4) * 2 + c
        arrived(slot)
        send(all_ref.at[:, slot], slot, sib)
    for d in (0, 3, 1, 2):
        arrived(((x + d) % 4) * 2 + 1 - c)
    mine.wait()
    for copy in sent:
        copy.wait_send()


def gather_head(own):
    return pl.pallas_call(
        gather_kernel,
        name="gather_input",
        out_shape=jax.ShapeDtypeStruct((3, HEADS) + own.shape[1:], own.dtype),
        in_specs=[VMEM],
        out_specs=VMEM,
        scratch_shapes=[
            pltpu.SemaphoreType.DMA((7,)),
            pltpu.SemaphoreType.DMA((HEADS,)),
            pltpu.SemaphoreType.DMA(()),
        ],
        compiler_params=pltpu.CompilerParams(collective_id=0, has_side_effects=True),
    )(own)


def delta_kernel(qk_ref, vz_ref, ba_ref, rate_ref, gain_ref, st_ref, out_ref):
    def unit(v):
        return v * lax.rsqrt(jnp.sum(v * v, axis=-1, keepdims=True) + EPS)

    q = unit(silu(qk_ref[0])) * (128 ** -0.5)
    k = unit(silu(qk_ref[1]))
    left = jnp.concatenate([k.reshape(24, 128), q.reshape(24, 128)], axis=0)
    place = lax.broadcasted_iota(jnp.int32, (48, 128), 0) % 8
    left = jnp.concatenate([jnp.where(place == s, left, 0.0) for s in range(8)], axis=1)
    st = st_ref[...]
    right = jnp.concatenate(
        [st[:, 0].reshape(1024, 128), st[:, 1].reshape(1024, 128)], axis=1
    ).astype(BF16)
    met = jnp.dot(left.astype(BF16), right, preferred_element_type=F32)
    ba = ba_ref[...]
    kk = {(i, t): jnp.sum(k[i] * k[t], axis=-1, keepdims=True) for i in range(3) for t in range(i + 1, 3)}
    kq = {(i, t): jnp.sum(k[i] * q[t], axis=-1, keepdims=True) for i in range(3) for t in range(i, 3)}
    for j in range(2):
        lane = slice(128 * j, 128 * j + 128)
        raw = ba[:, :, 2 + j : 3 + j] + rate_ref[1:2, j : j + 1]
        decay = jnp.exp(-jnp.exp(rate_ref[0:1, j : j + 1]) * jax.nn.softplus(raw))
        beta = jax.nn.sigmoid(ba[:, :, j : j + 1])
        deltas = []
        for t in range(3):
            whole = decay[0]
            for i in range(1, t + 1):
                whole = whole * decay[i]
            recalled = whole * met[8 * t : 8 * t + 8, lane]
            readout = whole * met[24 + 8 * t : 32 + 8 * t, lane]
            fade = jnp.ones_like(whole)
            for i in range(t - 1, -1, -1):
                fade = fade * decay[i + 1]
                recalled = recalled + (fade * kk[i, t]) * deltas[i]
                readout = readout + (fade * kq[i, t]) * deltas[i]
            deltas.append(beta[t] * (silu(vz_ref[j, 0, t]) - recalled))
            readout = readout + kq[t, t] * deltas[t]
            gated = rms_scale(readout, gain_ref[0:1]) * silu(vz_ref[j, 1, t])
            out_ref[t, :, lane] = gated.astype(BF16)


def delta_steps(qk, vz, ba, rates, gain, states):
    return pl.pallas_call(
        delta_kernel,
        name="delta_steps",
        grid=(8,),
        out_shape=jax.ShapeDtypeStruct((3, 64, 256), BF16),
        in_specs=[
            pl.BlockSpec((2, 3, 8, 128), lambda g: (0, 0, g, 0)),
            pl.BlockSpec((2, 2, 3, 8, 128), lambda g: (0, 0, 0, g, 0)),
            pl.BlockSpec((3, 8, 4), lambda g: (0, g, 0)),
            pl.BlockSpec((2, 2), lambda g: (0, 0)),
            pl.BlockSpec((1, 128), lambda g: (0, 0)),
            pl.BlockSpec((8, 2, 128, 128), lambda g: (g, 0, 0, 0)),
        ],
        out_specs=pl.BlockSpec((3, 8, 256), lambda g: (0, g, 0)),
        compiler_params=pltpu.CompilerParams(vmem_limit_bytes=32 * 2**20),
    )(qk, vz, ba, rates, gain, states)


def greet_all(p):
    barrier = pltpu.get_barrier_semaphore()

    @pl.loop(1, DEVS)
    def _(i):
        pl.semaphore_signal(barrier, inc=1, device_id=spot((p + i) % DEVS), device_id_type=MESH)

    pl.semaphore_wait(barrier, DEVS - 1)


def spread(p, first, send, recv, send_sem, recv_sem):
    @pl.loop(0, 16)
    def _(i):
        to = first + i

        @pl.when(to != p)
        def _():
            pltpu.make_async_remote_copy(
                src_ref=send.at[to],
                dst_ref=recv.at[p],
                send_sem=send_sem,
                recv_sem=recv_sem,
                device_id=spot(to),
                device_id_type=MESH,
            ).start()

        @pl.when(to == p)
        def _():
            pltpu.make_async_copy(send.at[to], recv.at[p], recv_sem).start()


def take(ref, sem):
    most = ref.at[pl.ds(0, ref.shape[0] - 1)]
    pltpu.make_async_copy(most, most, sem).wait()


def slot_parts(index):
    return index // 16, (index // 4) % 4, (index // 2) % 2, index % 2


def order_matrix(flip):
    rows = lax.broadcasted_iota(jnp.int32, (256, 256), flip)
    cols = lax.broadcasted_iota(jnp.int32, (256, 256), 1 - flip)
    source, chunk, expert, rank = slot_parts(cols)
    return jnp.where(rows == chunk * 64 + expert * 32 + rank * 16 + source, 1.0, 0.0).astype(BF16)


def dispatch_kernel(
    part_ref, hid_ref, gain_ref, ids_ref, x_ref, resid_ref, slice_ref,
    rs, send, recv, psend, stacked, rs_send, rs_recv, p_send, p_recv, send_sem, recv_sem,
):
    b = lax.axis_index("batch")
    h = lax.axis_index("head")
    p = b * HEADS + h
    greet_all(p)
    for i in range(1, HEADS):
        to = (h + i) % HEADS
        pltpu.make_async_remote_copy(
            src_ref=part_ref.at[:, to], dst_ref=rs.at[h], send_sem=rs_send, recv_sem=rs_recv,
            device_id=(b, to), device_id_type=MESH,
        ).start()
    take(rs, rs_recv)
    total = part_ref[:, h].astype(F32)
    for i in range(1, HEADS):
        total = total + rs[(h + i) % HEADS].astype(F32)
    resid = (hid_ref[...].astype(F32) + total).astype(BF16)
    resid_ref[...] = resid
    post = rms_scale(resid.astype(F32), gain_ref[...].reshape(1, 1, 2048)).astype(BF16)
    for i in range(HEADS):
        psend[i] = post[:, :, 256 * i : 256 * i + 256]
    rows = post.astype(F32).reshape(24, 2048)
    blank = jnp.zeros((8, 512), F32)
    stacked[...] = jnp.concatenate(
        [v for j in range(4) for v in (rows[:, 512 * j : 512 * j + 512], blank)], axis=0
    ).astype(BF16)
    for i in range(1, HEADS):
        to = (h + i) % HEADS
        pltpu.make_async_remote_copy(
            src_ref=psend.at[to], dst_ref=slice_ref.at[h], send_sem=p_send, recv_sem=p_recv,
            device_id=(b, to), device_id_type=MESH,
        ).start()
    slice_ref[h] = psend[h]
    i0 = lax.broadcasted_iota(jnp.int32, (128, 128), 0)
    i1 = lax.broadcasted_iota(jnp.int32, (128, 128), 1)
    earlier = jnp.where((i0 // 32 == i1 // 32) & (i0 < i1), 1.0, 0.0).astype(BF16)
    row = lax.broadcasted_iota(jnp.int32, (256, 128), 0)
    lane_chunk = lax.broadcasted_iota(jnp.int32, (256, 128), 1) // 32
    owner, chunk, expert, rank = slot_parts(row)
    named = owner * 2 + expert

    @pl.loop(0, 8)
    def _(i):
        group = (p // 16 + i) % 8
        here = named + group * 32
        hot = jnp.zeros((256, 128), F32)
        for k in range(10):
            hot = hot + jnp.where(ids_ref[k : k + 1, :] == here, 1.0, 0.0)
        before = jnp.dot(hot.astype(BF16), earlier, preferred_element_type=F32)
        chosen = (before == rank.astype(F32)) & (lane_chunk == chunk)
        placing = jnp.where(chosen, hot, 0.0).astype(BF16)
        rows = jnp.dot(placing, stacked[...], preferred_element_type=F32).astype(BF16)
        send[pl.ds(group * 16, 16)] = rows.reshape(16, 16, 512)
        spread(p, group * 16, send, recv, send_sem, recv_sem)

    order = order_matrix(0)
    pltpu.make_async_copy(recv, recv, recv_sem).wait()
    for g in range(8):
        got = recv[16 * g : 16 * g + 16].reshape(256, 512)
        got = jnp.dot(order, got, preferred_element_type=F32).astype(BF16)
        for j in range(4):
            for e in range(2):
                at = j * 64 + e * 32
                x_ref[e, 32 * g : 32 * g + 32, 512 * j : 512 * j + 512] = got[at : at + 32]
    take(psend, p_recv)
    take(rs, rs_send)
    take(psend, p_send)
    take(send, send_sem)


def dispatch(part, hid, gain, ids):
    return pl.pallas_call(
        dispatch_kernel,
        name="dispatch",
        out_shape=(
            jax.ShapeDtypeStruct((2, 256, 2048), BF16),
            jax.ShapeDtypeStruct((3, 8, 2048), BF16),
            jax.ShapeDtypeStruct((HEADS, 3, 8, 256), BF16),
        ),
        in_specs=[VMEM] * 4,
        out_specs=(VMEM,) * 3,
        scratch_shapes=[
            pltpu.VMEM((HEADS, 3, 8, 2048), BF16),
            pltpu.VMEM((DEVS, 16, 512), BF16),
            pltpu.VMEM((DEVS, 16, 512), BF16),
            pltpu.VMEM((HEADS, 3, 8, 256), BF16),
            pltpu.VMEM((128, 512), BF16),
        ]
        + [pltpu.SemaphoreType.DMA(())] * 6,
        compiler_params=pltpu.CompilerParams(
            collective_id=1, has_side_effects=True, vmem_limit_bytes=40 * 2**20
        ),
    )(part, hid, gain, ids)


def return_kernel(
    y_ref, sp_ref, ids_ref, w_ref, resid_ref, down_ref, out_ref,
    send, recv, sp_recv, mids, pair, pairs, gs, gr, ms, mr, ps, pr, send_sem, recv_sem,
):
    b = lax.axis_index("batch")
    h = lax.axis_index("head")
    p = b * HEADS + h
    greet_all(p)

    def to_heads(src, dst, ssem, rsem):
        for i in range(1, HEADS):
            to = (h + i) % HEADS
            pltpu.make_async_remote_copy(
                src_ref=src(to), dst_ref=dst.at[h], send_sem=ssem, recv_sem=rsem,
                device_id=(b, to), device_id_type=MESH,
            ).start()

    to_heads(lambda to: sp_ref.at[to], sp_recv, gs, gr)
    order = order_matrix(1)

    @pl.loop(0, 8)
    def _(i):
        group = (p // 16 + i) % 8
        at = pl.multiple_of(group * 32, 32)
        rows = jnp.concatenate(
            [y_ref[e, pl.ds(at, 32), 512 * j : 512 * j + 512] for j in range(4) for e in range(2)],
            axis=0,
        )
        rows = jnp.dot(order, rows, preferred_element_type=F32).astype(BF16)
        send[pl.ds(group * 16, 16)] = rows.reshape(16, 16, 512)
        spread(p, group * 16, send, recv, send_sem, recv_sem)

    take(sp_recv, gr)
    total = sp_ref[h].astype(F32)
    for i in range(1, HEADS):
        total = total + sp_recv[(h + i) % HEADS].astype(F32)
    logit = total[:, :, 1024:1025] + total[:, :, 1025:1026]
    mid = silu(total[:, :, :512]) * total[:, :, 512:1024] * jax.nn.sigmoid(logit)
    mids[h] = mid.astype(BF16)
    to_heads(lambda to: mids.at[h], mids, ms, mr)

    i0 = lax.broadcasted_iota(jnp.int32, (128, 128), 0)
    i1 = lax.broadcasted_iota(jnp.int32, (128, 128), 1)
    earlier = jnp.where((i0 // 32 == i1 // 32) & (i1 < i0), 1.0, 0.0).astype(BF16)
    col = lax.broadcasted_iota(jnp.int32, (128, 256), 1)
    row_chunk = lax.broadcasted_iota(jnp.int32, (128, 256), 0) // 32
    owner, chunk, expert, rank = slot_parts(col)
    named = owner * 2 + expert

    def weights(g):
        here = named + g * 32
        hot = jnp.zeros((128, 256), F32)
        load = jnp.zeros((128, 256), F32)
        for k in range(10):
            same = ids_ref[:, k : k + 1] == here
            hot = hot + jnp.where(same, 1.0, 0.0)
            load = load + jnp.where(same, w_ref[:, k : k + 1], 0.0)
        before = jnp.dot(earlier, hot.astype(BF16), preferred_element_type=F32)
        load = jnp.where((before == rank.astype(F32)) & (row_chunk == chunk), load, 0.0)
        high = load.astype(BF16)
        return jnp.concatenate([high, (load - high.astype(F32)).astype(BF16)], axis=0)

    load = [weights(g) for g in range(8)]
    pltpu.make_async_copy(recv, recv, recv_sem).wait()
    acc = jnp.zeros((256, 512), F32)
    for g in range(8):
        got = recv[16 * g : 16 * g + 16].reshape(256, 512)
        acc = acc + jnp.dot(load[g], got, preferred_element_type=F32)
    acc = acc[:128] + acc[128:]
    routed = jnp.concatenate([acc[32 * j : 32 * j + 24] for j in range(4)], axis=1)
    routed = routed.reshape(3, 8, 2048).astype(BF16)
    for i in range(HEADS):
        pair[i, 0] = resid_ref[:, :, 256 * i : 256 * i + 256]
        pair[i, 1] = routed[:, :, 256 * i : 256 * i + 256]
    to_heads(lambda to: pair.at[to], pairs, ps, pr)
    pairs[h] = pair[h]
    take(mids, mr)
    every = mids[...].astype(F32).reshape(192, 512).astype(BF16)
    shared = jnp.dot(every, down_ref[...], preferred_element_type=F32).reshape(HEADS, 3, 8, 256)
    take(pairs, pr)
    for o in range(HEADS):
        both = pairs[o].astype(F32)
        out_ref[:, o] = (both[0] + shared[o] + both[1]).astype(BF16)
    take(sp_recv, gs)
    take(mids, ms)
    take(pairs, ps)
    take(send, send_sem)


def give_back(y, sp, ids, w, resid, down):
    return pl.pallas_call(
        return_kernel,
        name="give_back",
        out_shape=jax.ShapeDtypeStruct((3, HEADS, 8, 256), BF16),
        in_specs=[VMEM] * 6,
        out_specs=VMEM,
        scratch_shapes=[
            pltpu.VMEM((DEVS, 16, 512), BF16),
            pltpu.VMEM((DEVS, 16, 512), BF16),
            pltpu.VMEM((HEADS, 3, 8, 1152), BF16),
            pltpu.VMEM((HEADS, 3, 8, 512), BF16),
            pltpu.VMEM((HEADS, 2, 3, 8, 256), BF16),
            pltpu.VMEM((HEADS, 2, 3, 8, 256), BF16),
        ]
        + [pltpu.SemaphoreType.DMA(())] * 8,
        compiler_params=pltpu.CompilerParams(
            collective_id=2, has_side_effects=True, vmem_limit_bytes=40 * 2**20
        ),
    )(y, sp, ids, w, resid, down)


def shards(
    hidden_in, states, norm_in, w_qk, w_vz, w_ba, a_log, dt_bias, norm_gate, w_out, norm_post,
    shared_in, shared_gate, shared_out, expert_in, expert_out, routes, route_weight,
):
    hid = hidden_in.transpose(1, 0, 2)
    ids = routes.transpose(1, 0, 2).reshape(24, 10)
    ids = jnp.pad(ids, ((0, 8), (0, 6)), constant_values=-1)
    ids = jnp.tile(ids, (4, 1))
    load = route_weight.transpose(1, 0, 2).reshape(24, 10)
    load = jnp.tile(jnp.pad(load, ((0, 8), (0, 6))), (4, 1))
    gathered = gather_head(hid).reshape(192, 2048)
    normed = rms_scale(gathered.astype(F32), norm_in).astype(BF16)
    qk = jnp.einsum("nd,dhck->chnk", normed, w_qk, preferred_element_type=F32)
    vz = jnp.einsum("nd,dhcv->hcnv", normed, w_vz, preferred_element_type=F32)
    ba = jnp.einsum("nd,dch->nch", normed, w_ba, preferred_element_type=F32)
    gated = delta_steps(
        qk.reshape(2, 3, 64, 128),
        vz.reshape(2, 2, 3, 64, 128),
        ba.reshape(3, 64, 4),
        jnp.stack([a_log, dt_bias]),
        norm_gate.reshape(1, 128),
        states,
    )
    part = jnp.dot(
        gated.reshape(192, 256), w_out.reshape(256, 2048), preferred_element_type=F32
    ).astype(BF16)
    x, resid, slices = dispatch(
        part.reshape(3, HEADS, 8, 2048), hid, norm_post.reshape(1, 2048), ids.T
    )
    gate_up = jnp.einsum("xnd,xdgf->xngf", x, expert_in, preferred_element_type=F32)
    inner = (silu(gate_up[:, :, 0]) * gate_up[:, :, 1]).astype(BF16)
    y = jnp.einsum("xnf,xfd->xnd", inner, expert_out, preferred_element_type=F32).astype(BF16)
    slices = slices.reshape(192, 256)
    up = jnp.einsum("nd,dcf->ncf", slices, shared_in, preferred_element_type=F32)
    logit = jnp.einsum("nd,d->n", slices, shared_gate, preferred_element_type=F32)[:, None]
    high = logit.astype(BF16)
    low = (logit - high.astype(F32)).astype(BF16)
    sp = jnp.concatenate(
        [up.reshape(192, 1024).astype(BF16), high, low, jnp.zeros((192, 126), BF16)], axis=1
    )
    out = give_back(y, sp.reshape(HEADS, 3, 8, 1152), ids, load, resid, shared_out)
    return out.reshape(3, 64, 256).transpose(1, 0, 2)


def solution(mesh):
    in_specs = (
        P(("batch", "head"), None, None),
        P("batch", "head", None, None),
        P(),
        P(None, "head", None, None),
        P(None, "head", None, None),
        P(None, None, "head"),
        P("head"),
        P("head"),
        P(),
        P("head", None, None),
        P(),
        P("head", None, None),
        P("head"),
        P(None, "head"),
        P(("batch", "head"), None, None, None),
        P(("batch", "head"), None, None),
        P(("batch", "head"), None, None),
        P(("batch", "head"), None, None),
    )
    out_specs = P("batch", None, "head")
    return jax.shard_map(shards, mesh=mesh, in_specs=in_specs, out_specs=out_specs, check_vma=False)
```

```python
import functools

import jax
import jax.numpy as jnp
from jax import lax
from jax.experimental import pallas as pl
from jax.experimental.pallas import tpu as pltpu
from jax.sharding import PartitionSpec as P

EPS = 1e-06
MESH = pl.DeviceIdType.MESH
HEADS = 8
BATCH = 16
DEVS = HEADS * BATCH
F32 = jnp.float32
BF16 = jnp.bfloat16
VMEM = pl.BlockSpec(memory_space=pltpu.VMEM)


def rms_scale(values, gain):
    return values * lax.rsqrt(jnp.mean(values * values, axis=-1, keepdims=True) + EPS) * gain


def silu(v):
    return v * jax.nn.sigmoid(v)


def spot(p):
    return (p // HEADS, p % HEADS)


def gather_kernel(own_ref, all_ref, send_sem, recv_sem, local_sem):
    b = lax.axis_index("batch")
    h = lax.axis_index("head")
    x, c = h // 2, h % 2
    sib = x * 2 + 1 - c
    chips = [(x + d) % 4 for d in (1, 3, 2)]
    barrier = pltpu.get_barrier_semaphore()
    for to in [sib] + [v * 2 + c for v in chips]:
        pl.semaphore_signal(barrier, inc=1, device_id=(b, to), device_id_type=MESH)
    pl.semaphore_wait(barrier, 4)
    mine = pltpu.make_async_copy(own_ref, all_ref.at[:, h], local_sem)
    mine.start()
    sent = []

    def send(src, slot, to):
        copy = pltpu.make_async_remote_copy(
            src_ref=src,
            dst_ref=all_ref.at[:, slot],
            send_sem=send_sem.at[len(sent)],
            recv_sem=recv_sem.at[slot],
            device_id=(b, to),
            device_id_type=MESH,
        )
        copy.start()
        sent.append(copy)

    def arrived(slot):
        pltpu.make_async_copy(own_ref, all_ref.at[:, slot], recv_sem.at[slot]).wait()

    for v in chips:
        send(own_ref, h, v * 2 + c)
    send(own_ref, h, sib)
    for d in (3, 1, 2):
        slot = ((x + d) % 4) * 2 + c
        arrived(slot)
        send(all_ref.at[:, slot], slot, sib)
    for d in (0, 3, 1, 2):
        arrived(((x + d) % 4) * 2 + 1 - c)
    mine.wait()
    for copy in sent:
        copy.wait_send()


def gather_head(own):
    return pl.pallas_call(
        gather_kernel,
        name="gather_input",
        out_shape=jax.ShapeDtypeStruct((3, HEADS) + own.shape[1:], own.dtype),
        in_specs=[VMEM],
        out_specs=VMEM,
        scratch_shapes=[
            pltpu.SemaphoreType.DMA((7,)),
            pltpu.SemaphoreType.DMA((HEADS,)),
            pltpu.SemaphoreType.DMA(()),
        ],
        compiler_params=pltpu.CompilerParams(collective_id=0, has_side_effects=True),
    )(own)


def delta_kernel(qk_ref, vz_ref, ba_ref, rate_ref, gain_ref, st_ref, out_ref):
    def unit(v):
        return v * lax.rsqrt(jnp.sum(v * v, axis=-1, keepdims=True) + EPS)

    q = unit(silu(qk_ref[0])) * (128 ** -0.5)
    k = unit(silu(qk_ref[1]))
    left = jnp.concatenate([k.reshape(24, 128), q.reshape(24, 128)], axis=0)
    place = lax.broadcasted_iota(jnp.int32, (48, 128), 0) % 8
    left = jnp.concatenate([jnp.where(place == s, left, 0.0) for s in range(8)], axis=1)
    st = st_ref[...]
    right = jnp.concatenate(
        [st[:, 0].reshape(1024, 128), st[:, 1].reshape(1024, 128)], axis=1
    ).astype(BF16)
    met = jnp.dot(left.astype(BF16), right, preferred_element_type=F32)
    ba = ba_ref[...]
    kk = {(i, t): jnp.sum(k[i] * k[t], axis=-1, keepdims=True) for i in range(3) for t in range(i + 1, 3)}
    kq = {(i, t): jnp.sum(k[i] * q[t], axis=-1, keepdims=True) for i in range(3) for t in range(i, 3)}
    for j in range(2):
        lane = slice(128 * j, 128 * j + 128)
        raw = ba[:, :, 2 + j : 3 + j] + rate_ref[1:2, j : j + 1]
        decay = jnp.exp(-jnp.exp(rate_ref[0:1, j : j + 1]) * jax.nn.softplus(raw))
        beta = jax.nn.sigmoid(ba[:, :, j : j + 1])
        deltas = []
        for t in range(3):
            whole = decay[0]
            for i in range(1, t + 1):
                whole = whole * decay[i]
            recalled = whole * met[8 * t : 8 * t + 8, lane]
            readout = whole * met[24 + 8 * t : 32 + 8 * t, lane]
            fade = jnp.ones_like(whole)
            for i in range(t - 1, -1, -1):
                fade = fade * decay[i + 1]
                recalled = recalled + (fade * kk[i, t]) * deltas[i]
                readout = readout + (fade * kq[i, t]) * deltas[i]
            deltas.append(beta[t] * (silu(vz_ref[j, 0, t]) - recalled))
            readout = readout + kq[t, t] * deltas[t]
            gated = rms_scale(readout, gain_ref[0:1]) * silu(vz_ref[j, 1, t])
            out_ref[t, :, lane] = gated.astype(BF16)


def delta_steps(qk, vz, ba, rates, gain, states):
    return pl.pallas_call(
        delta_kernel,
        name="delta_steps",
        grid=(8,),
        out_shape=jax.ShapeDtypeStruct((3, 64, 256), BF16),
        in_specs=[
            pl.BlockSpec((2, 3, 8, 128), lambda g: (0, 0, g, 0)),
            pl.BlockSpec((2, 2, 3, 8, 128), lambda g: (0, 0, 0, g, 0)),
            pl.BlockSpec((3, 8, 4), lambda g: (0, g, 0)),
            pl.BlockSpec((2, 2), lambda g: (0, 0)),
            pl.BlockSpec((1, 128), lambda g: (0, 0)),
            pl.BlockSpec((8, 2, 128, 128), lambda g: (g, 0, 0, 0)),
        ],
        out_specs=pl.BlockSpec((3, 8, 256), lambda g: (0, g, 0)),
        compiler_params=pltpu.CompilerParams(vmem_limit_bytes=32 * 2**20),
    )(qk, vz, ba, rates, gain, states)


def greet_all(p):
    barrier = pltpu.get_barrier_semaphore()

    @pl.loop(1, DEVS)
    def _(i):
        pl.semaphore_signal(barrier, inc=1, device_id=spot((p + i) % DEVS), device_id_type=MESH)

    pl.semaphore_wait(barrier, DEVS - 1)


def spread(p, first, send, recv, send_sem, recv_sem):
    @pl.loop(0, 16)
    def _(i):
        to = first + i

        @pl.when(to != p)
        def _():
            pltpu.make_async_remote_copy(
                src_ref=send.at[to],
                dst_ref=recv.at[p],
                send_sem=send_sem,
                recv_sem=recv_sem,
                device_id=spot(to),
                device_id_type=MESH,
            ).start()

        @pl.when(to == p)
        def _():
            pltpu.make_async_copy(send.at[to], recv.at[p], recv_sem).start()


def take(ref, sem):
    most = ref.at[pl.ds(0, ref.shape[0] - 1)]
    pltpu.make_async_copy(most, most, sem).wait()


def slot_parts(index):
    return index // 16, (index // 4) % 4, (index // 2) % 2, index % 2


def order_matrix(flip):
    rows = lax.broadcasted_iota(jnp.int32, (256, 256), flip)
    cols = lax.broadcasted_iota(jnp.int32, (256, 256), 1 - flip)
    source, chunk, expert, rank = slot_parts(cols)
    return jnp.where(rows == chunk * 64 + expert * 32 + rank * 16 + source, 1.0, 0.0).astype(BF16)


def part_rows(raw, wide, blocks):
    rows = lax.broadcasted_iota(jnp.int32, (256, 256), 0)
    cols = lax.broadcasted_iota(jnp.int32, (256, 256), 1)
    order = jnp.where(cols == (rows % 32) * 8 + rows // 32, 1.0, 0.0).astype(BF16)

    @pl.loop(0, blocks)
    def _(i):
        at = pl.multiple_of(i * 512, 512)
        to = pl.multiple_of(i * 64, 64)
        pair = jnp.concatenate([raw[pl.ds(at, 256)], raw[pl.ds(at + 256, 256)]], axis=1)
        got = jnp.dot(order, pair, preferred_element_type=F32).astype(BF16)
        for s in range(8):
            lane = (s % 2) * 512 + (s // 2) * 128
            part = got[32 * s : 32 * s + 32]
            wide[pl.ds(to, 32), lane : lane + 128] = part[:, :128]
            wide[pl.ds(to + 32, 32), lane : lane + 128] = part[:, 128:]


def moe_kernel(
    part_ref, hid_ref, gain_ref, idt_ref, ids_ref, w_ref, sraw_ref, sgate_ref, down_ref, win_ref, wout_ref,
    out_ref,
    rs, send, recv, psend, slices, stacked, placing, load, raw, win, wout, swin, xs, ys,
    back, home, sp, sp_recv, mids, pair, pairs,
    rs_s, rs_r, p_s, p_r, d_s, d_r, b_s, b_r, g_s, g_r, m_s, m_r, q_s, q_r, win_sem, wout_sem,
):
    b = lax.axis_index("batch")
    h = lax.axis_index("head")
    p = b * HEADS + h
    mine = p // 16

    def to_heads(src, dst, ssem, rsem):
        for i in range(1, HEADS):
            to = (h + i) % HEADS
            pltpu.make_async_remote_copy(
                src_ref=src(to), dst_ref=dst.at[h], send_sem=ssem, recv_sem=rsem,
                device_id=(b, to), device_id_type=MESH,
            ).start()

    win_copy = pltpu.make_async_copy(win_ref, raw, win_sem)
    win_copy.start()
    wout_copy = pltpu.make_async_copy(wout_ref, wout, wout_sem)
    wout_copy.start()
    greet_all(p)
    to_heads(lambda to: part_ref.at[:, to], rs, rs_s, rs_r)

    i0 = lax.broadcasted_iota(jnp.int32, (128, 128), 0)
    i1 = lax.broadcasted_iota(jnp.int32, (128, 128), 1)
    earlier = jnp.where((i0 // 32 == i1 // 32) & (i0 < i1), 1.0, 0.0).astype(BF16)
    later = jnp.where((i0 // 32 == i1 // 32) & (i1 < i0), 1.0, 0.0).astype(BF16)
    lane_chunk = lax.broadcasted_iota(jnp.int32, (256, 128), 1) // 32
    owner, chunk, expert, rank = slot_parts(lax.broadcasted_iota(jnp.int32, (256, 128), 0))
    named = owner * 2 + expert

    @pl.loop(0, 8)
    def _(g):
        here = named + g * 32
        hot = jnp.zeros((256, 128), F32)
        for k in range(10):
            hot = hot + jnp.where(idt_ref[k : k + 1, :] == here, 1.0, 0.0)
        before = jnp.dot(hot.astype(BF16), earlier, preferred_element_type=F32)
        chosen = (before == rank.astype(F32)) & (lane_chunk == chunk)
        placing[g] = jnp.where(chosen, hot, 0.0).astype(BF16)

    part_rows(sraw_ref, swin, 4)
    win_copy.wait()
    part_rows(raw, win, 64)

    take(rs, rs_r)
    total = part_ref[:, h].astype(F32)
    for i in range(1, HEADS):
        total = total + rs[(h + i) % HEADS].astype(F32)
    resid = (hid_ref[...].astype(F32) + total).astype(BF16)
    post = rms_scale(resid.astype(F32), gain_ref[...].reshape(1, 1, 2048)).astype(BF16)
    for i in range(HEADS):
        psend[i] = post[:, :, 256 * i : 256 * i + 256]
        pair[i, 0] = resid[:, :, 256 * i : 256 * i + 256]
    to_heads(lambda to: psend.at[to], slices, p_s, p_r)
    slices[h] = psend[h]
    rows = post.astype(F32).reshape(24, 2048)
    blank = jnp.zeros((8, 512), F32)
    stacked[...] = jnp.concatenate(
        [v for j in range(4) for v in (rows[:, 512 * j : 512 * j + 512], blank)], axis=0
    ).astype(BF16)

    @pl.loop(0, 8)
    def _(i):
        group = (mine + i) % 8
        rows = jnp.dot(placing[group], stacked[...], preferred_element_type=F32).astype(BF16)
        send[pl.ds(group * 16, 16)] = rows.reshape(16, 16, 512)
        spread(p, group * 16, send, recv, d_s, d_r.at[mine])

    take(psend, p_r)
    every = slices[...].astype(F32).reshape(192, 256)
    up = jnp.dot(every.astype(BF16), swin[...], preferred_element_type=F32)
    logit = jnp.sum(every * sgate_ref[...].astype(F32), axis=-1, keepdims=True)
    high = logit.astype(BF16).astype(F32)
    zero = jnp.zeros((192, 126), F32)
    sp[...] = (
        jnp.concatenate([up, high, logit - high, zero], axis=1).astype(BF16).reshape(HEADS, 3, 8, 1152)
    )
    to_heads(lambda to: sp.at[to], sp_recv, g_s, g_r)

    row_chunk = lax.broadcasted_iota(jnp.int32, (128, 256), 0) // 32
    owner2, chunk2, expert2, rank2 = slot_parts(lax.broadcasted_iota(jnp.int32, (128, 256), 1))
    named2 = owner2 * 2 + expert2

    @pl.loop(0, 8)
    def _(g):
        here = named2 + g * 32
        hot = jnp.zeros((128, 256), F32)
        heavy = jnp.zeros((128, 256), F32)
        for k in range(10):
            same = ids_ref[:, k : k + 1] == here
            hot = hot + jnp.where(same, 1.0, 0.0)
            heavy = heavy + jnp.where(same, w_ref[:, k : k + 1], 0.0)
        before = jnp.dot(later, hot.astype(BF16), preferred_element_type=F32)
        heavy = jnp.where((before == rank2.astype(F32)) & (row_chunk == chunk2), heavy, 0.0)
        top = heavy.astype(BF16)
        load[g, :128] = top
        load[g, 128:] = (heavy - top.astype(F32)).astype(BF16)

    wout_copy.wait()
    order = order_matrix(0)
    undo = order_matrix(1)
    for half in range(2):
        @pl.loop(0, 4)
        def _(i):
            group = (mine + 8 - (4 * half + i)) % 8
            blocks = recv.at[pl.ds(group * 16, 16)]
            pltpu.make_async_copy(blocks, blocks, d_r.at[group]).wait()
            got = recv[pl.ds(group * 16, 16)].reshape(256, 512)
            got = jnp.dot(order, got, preferred_element_type=F32).astype(BF16)
            to = pl.multiple_of(i * 32, 32)
            for j in range(4):
                for e in range(2):
                    at = j * 64 + e * 32
                    xs[e, pl.ds(to, 32), 512 * j : 512 * j + 512] = got[at : at + 32]

        @pl.loop(0, 2)
        def _(e):
            inner = []
            for n in range(2):
                lane = slice(256 * n, 256 * n + 256)
                lane2 = slice(512 + 256 * n, 768 + 256 * n)
                gate = jnp.dot(xs[e], win[pl.ds(e * 2048, 2048), lane], preferred_element_type=F32)
                more = jnp.dot(xs[e], win[pl.ds(e * 2048, 2048), lane2], preferred_element_type=F32)
                inner.append((silu(gate) * more).astype(BF16))
            inner = jnp.concatenate(inner, axis=1)
            for j in range(4):
                lane = slice(512 * j, 512 * j + 512)
                ys[e, :, lane] = jnp.dot(inner, wout[e, :, lane], preferred_element_type=F32).astype(BF16)

        @pl.loop(0, 4)
        def _(i):
            group = (mine + 8 - (4 * half + i)) % 8
            at = pl.multiple_of(i * 32, 32)
            rows = jnp.concatenate(
                [ys[e, pl.ds(at, 32), 512 * j : 512 * j + 512] for j in range(4) for e in range(2)],
                axis=0,
            )
            rows = jnp.dot(undo, rows, preferred_element_type=F32).astype(BF16)
            back[pl.ds(group * 16, 16)] = rows.reshape(16, 16, 512)
            spread(p, group * 16, back, home, b_s, b_r)

        if half == 0:
            take(sp_recv, g_r)
            total = sp[h].astype(F32)
            for i in range(1, HEADS):
                total = total + sp_recv[(h + i) % HEADS].astype(F32)
            logit = total[:, :, 1024:1025] + total[:, :, 1025:1026]
            mid = silu(total[:, :, :512]) * total[:, :, 512:1024] * jax.nn.sigmoid(logit)
            mids[h] = mid.astype(BF16)
            to_heads(lambda to: mids.at[h], mids, m_s, m_r)

    take(mids, m_r)
    every = mids[...].astype(F32).reshape(192, 512).astype(BF16)
    shared = jnp.dot(every, down_ref[...], preferred_element_type=F32).reshape(HEADS, 3, 8, 256)
    pltpu.make_async_copy(home, home, b_r).wait()
    acc = jnp.zeros((256, 512), F32)
    for g in range(8):
        got = home[16 * g : 16 * g + 16].reshape(256, 512)
        acc = acc + jnp.dot(load[g], got, preferred_element_type=F32)
    acc = acc[:128] + acc[128:]
    routed = jnp.concatenate([acc[32 * j : 32 * j + 24] for j in range(4)], axis=1)
    routed = routed.reshape(3, 8, 2048).astype(BF16)
    for i in range(HEADS):
        pair[i, 1] = routed[:, :, 256 * i : 256 * i + 256]
    to_heads(lambda to: pair.at[to], pairs, q_s, q_r)
    pairs[h] = pair[h]
    take(pairs, q_r)
    for o in range(HEADS):
        both = pairs[o].astype(F32)
        out_ref[:, o] = (both[0] + shared[o] + both[1]).astype(BF16)
    take(rs, rs_s)
    take(psend, p_s)
    take(send, d_s)
    take(sp, g_s)
    take(mids, m_s)
    take(back, b_s)
    take(pairs, q_s)


def moe(*args):
    any_place = pl.BlockSpec(memory_space=pl.ANY)
    return pl.pallas_call(
        moe_kernel,
        name="moe",
        out_shape=jax.ShapeDtypeStruct((3, HEADS, 8, 256), BF16),
        in_specs=[VMEM] * 9 + [any_place] * 2,
        out_specs=VMEM,
        scratch_shapes=[
            pltpu.VMEM((HEADS, 3, 8, 2048), BF16),
            pltpu.VMEM((DEVS, 16, 512), BF16),
            pltpu.VMEM((DEVS, 16, 512), BF16),
            pltpu.VMEM((HEADS, 3, 8, 256), BF16),
            pltpu.VMEM((HEADS, 3, 8, 256), BF16),
            pltpu.VMEM((128, 512), BF16),
            pltpu.VMEM((8, 256, 128), BF16),
            pltpu.VMEM((8, 256, 256), BF16),
            pltpu.VMEM((32768, 128), BF16),
            pltpu.VMEM((4096, 1024), BF16),
            pltpu.VMEM((2, 512, 2048), BF16),
            pltpu.VMEM((256, 1024), BF16),
            pltpu.VMEM((2, 128, 2048), BF16),
            pltpu.VMEM((2, 128, 2048), BF16),
            pltpu.VMEM((DEVS, 16, 512), BF16),
            pltpu.VMEM((DEVS, 16, 512), BF16),
            pltpu.VMEM((HEADS, 3, 8, 1152), BF16),
            pltpu.VMEM((HEADS, 3, 8, 1152), BF16),
            pltpu.VMEM((HEADS, 3, 8, 512), BF16),
            pltpu.VMEM((HEADS, 2, 3, 8, 256), BF16),
            pltpu.VMEM((HEADS, 2, 3, 8, 256), BF16),
        ]
        + [pltpu.SemaphoreType.DMA(())] * 5
        + [pltpu.SemaphoreType.DMA((8,))]
        + [pltpu.SemaphoreType.DMA(())] * 10,
        compiler_params=pltpu.CompilerParams(
            collective_id=1, has_side_effects=True, vmem_limit_bytes=56 * 2**20
        ),
    )(*args)


def column_rows(w):
    return w.reshape(-1, 2, 4, 128).transpose(0, 2, 1, 3).reshape(-1, 128)


def shards(
    hidden_in, states, norm_in, w_qk, w_vz, w_ba, a_log, dt_bias, norm_gate, w_out, norm_post,
    shared_in, shared_gate, shared_out, expert_in, expert_out, routes, route_weight,
):
    hid = hidden_in.transpose(1, 0, 2)
    ids = routes.transpose(1, 0, 2).reshape(24, 10)
    ids = jnp.pad(ids, ((0, 8), (0, 6)), constant_values=-1)
    ids = jnp.tile(ids, (4, 1))
    load = route_weight.transpose(1, 0, 2).reshape(24, 10)
    load = jnp.tile(jnp.pad(load, ((0, 8), (0, 6))), (4, 1))
    gathered = gather_head(hid).reshape(192, 2048)
    normed = rms_scale(gathered.astype(F32), norm_in).astype(BF16)
    qk = jnp.einsum("nd,dhck->chnk", normed, w_qk, preferred_element_type=F32)
    vz = jnp.einsum("nd,dhcv->hcnv", normed, w_vz, preferred_element_type=F32)
    ba = jnp.einsum("nd,dch->nch", normed, w_ba, preferred_element_type=F32)
    gated = delta_steps(
        qk.reshape(2, 3, 64, 128),
        vz.reshape(2, 2, 3, 64, 128),
        ba.reshape(3, 64, 4),
        jnp.stack([a_log, dt_bias]),
        norm_gate.reshape(1, 128),
        states,
    )
    part = jnp.dot(
        gated.reshape(192, 256), w_out.reshape(256, 2048), preferred_element_type=F32
    ).astype(BF16)
    out = moe(
        part.reshape(3, HEADS, 8, 2048),
        hid,
        norm_post.reshape(1, 2048),
        ids.T,
        ids,
        load,
        column_rows(shared_in),
        shared_gate.reshape(1, 256),
        shared_out,
        column_rows(expert_in),
        expert_out,
    )
    return out.reshape(3, 64, 256).transpose(1, 0, 2)


def solution(mesh):
    in_specs = (
        P(("batch", "head"), None, None),
        P("batch", "head", None, None),
        P(),
        P(None, "head", None, None),
        P(None, "head", None, None),
        P(None, None, "head"),
        P("head"),
        P("head"),
        P(),
        P("head", None, None),
        P(),
        P("head", None, None),
        P("head"),
        P(None, "head"),
        P(("batch", "head"), None, None, None),
        P(("batch", "head"), None, None),
        P(("batch", "head"), None, None),
        P(("batch", "head"), None, None),
    )
    out_specs = P("batch", None, "head")
    return jax.shard_map(shards, mesh=mesh, in_specs=in_specs, out_specs=out_specs, check_vma=False)
```

```python
import jax
import jax.numpy as jnp
from jax import lax
from jax.experimental import pallas as pl
from jax.experimental.pallas import tpu as pltpu
from jax.sharding import PartitionSpec as P

EPS = 1e-06
MESH = pl.DeviceIdType.MESH
HEADS = 8
BATCH = 16
DEVS = HEADS * BATCH
F32 = jnp.float32
BF16 = jnp.bfloat16
VMEM = pl.BlockSpec(memory_space=pltpu.VMEM)
ANY = pl.BlockSpec(memory_space=pl.ANY)


def rms_scale(values, gain):
    return values * lax.rsqrt(jnp.mean(values * values, axis=-1, keepdims=True) + EPS) * gain


def unit_norm(v):
    return v * lax.rsqrt(jnp.sum(v * v, axis=-1, keepdims=True) + EPS)


def silu(v):
    return v * jax.nn.sigmoid(v)


def iota(shape, axis):
    return lax.broadcasted_iota(jnp.int32, shape, axis)


def mm(left, right):
    return jnp.dot(left, right, preferred_element_type=F32)


def one_hot(mask):
    return jnp.where(mask, 1.0, 0.0)


def spot(p):
    return (p // HEADS, p % HEADS)


def remote(src, dst, send_sem, recv_sem, to):
    return pltpu.make_async_remote_copy(
        src_ref=src, dst_ref=dst, send_sem=send_sem, recv_sem=recv_sem, device_id=to, device_id_type=MESH
    )


def wait_bytes(ref, sem):
    pltpu.make_async_copy(ref, ref, sem).wait()


def take(ref, sem):
    wait_bytes(ref.at[pl.ds(0, ref.shape[0] - 1)], sem)


def spread(p, first, send, recv, send_sem, recv_sem):
    @pl.loop(0, 16)
    def _(i):
        to = first + i

        @pl.when(to != p)
        def _():
            remote(send.at[to], recv.at[p], send_sem, recv_sem, spot(to)).start()

        @pl.when(to == p)
        def _():
            pltpu.make_async_copy(send.at[to], recv.at[p], recv_sem).start()


def part_rows(raw, wide, kinds, lane_of, blocks, from_row=0, to_row=0):
    count = 256 // kinds
    order = one_hot(iota((256, 256), 1) == (iota((256, 256), 0) % count) * kinds + iota((256, 256), 0) // count)
    order = order.astype(BF16)

    @pl.loop(0, blocks)
    def _(i):
        at = pl.multiple_of(from_row + i * 512, 512)
        to = pl.multiple_of(to_row + i * 2 * count, 2 * count)
        pair = jnp.concatenate([raw[pl.ds(at, 256)], raw[pl.ds(at + 256, 256)]], axis=1)
        got = mm(order, pair).astype(BF16)
        for s in range(kinds):
            lane = lane_of(s)
            part = got[count * s : count * s + count]
            wide[pl.ds(to, count), lane : lane + 128] = part[:, :128]
            wide[pl.ds(to + count, count), lane : lane + 128] = part[:, 128:]


def gate_up_lane(s):
    return (s % 2) * 512 + (s // 2) * 128


def count_hits(ids, here):
    hot = jnp.zeros(here.shape, F32)
    for k in range(10):
        hot = hot + one_hot(ids[:, k : k + 1] == here)
    return hot


def delta_rows(rows, ba, rates, gain, states):
    q = unit_norm(silu(rows[:, :128])) * (128 ** -0.5)
    k = unit_norm(silu(rows[:, 128:256]))
    left = jnp.concatenate([k, q], axis=0)
    place = iota((48, 128), 0) % 8
    left = jnp.concatenate([jnp.where(place == s, left, 0.0) for s in range(8)], axis=1)
    right = jnp.concatenate(
        [states[:, 0].reshape(1024, 128), states[:, 1].reshape(1024, 128)], axis=1
    ).astype(BF16)
    met = mm(left.astype(BF16), right)
    q = [q[8 * t : 8 * t + 8] for t in range(3)]
    k = [k[8 * t : 8 * t + 8] for t in range(3)]

    def along(u, v):
        return jnp.sum(u * v, axis=-1, keepdims=True)

    kk = {(i, t): along(k[i], k[t]) for i in range(3) for t in range(i + 1, 3)}
    kq = {(i, t): along(k[i], q[t]) for i in range(3) for t in range(i, 3)}
    heads = []
    for j in range(2):
        lane = slice(128 * j, 128 * j + 128)
        values = silu(rows[:, 256 + 256 * j : 384 + 256 * j])
        gate_z = silu(rows[:, 384 + 256 * j : 512 + 256 * j])
        raw = ba[:, 2 + j : 3 + j] + rates[1:2, j : j + 1]
        decays = jnp.exp(-jnp.exp(rates[0:1, j : j + 1]) * jax.nn.softplus(raw))
        betas = jax.nn.sigmoid(ba[:, j : j + 1])
        decay = [decays[8 * t : 8 * t + 8] for t in range(3)]
        deltas, steps = [], []
        for t in range(3):
            whole = decay[0]
            for i in range(1, t + 1):
                whole = whole * decay[i]
            recalled = whole * met[8 * t : 8 * t + 8, lane]
            readout = whole * met[24 + 8 * t : 32 + 8 * t, lane]
            fade = jnp.ones_like(whole)
            for i in range(t - 1, -1, -1):
                fade = fade * decay[i + 1]
                recalled = recalled + (fade * kk[i, t]) * deltas[i]
                readout = readout + (fade * kq[i, t]) * deltas[i]
            deltas.append(betas[8 * t : 8 * t + 8] * (values[8 * t : 8 * t + 8] - recalled))
            readout = readout + kq[t, t] * deltas[t]
            steps.append(rms_scale(readout, gain) * gate_z[8 * t : 8 * t + 8])
        heads.append(jnp.concatenate(steps, axis=0))
    return jnp.concatenate(heads, axis=1)


def layer_kernel(
    hid_ref, ids_ref, wt_ref, gain_in, rates_ref, gain_gate, gain_post, wba_ref, sgate_ref,
    states_hbm, wqk_hbm, wvz_hbm, wo_hbm, sraw_hbm, down_hbm, win_hbm, wout_hbm,
    out_ref,
    hall, nrm, proj, bas, states, wqk, wvz, wide, wo, sraw, swin, down, raw, win, wout,
    ids_all, wts_all, partb, rs, send, recv, psend, slices, stacked, placing, load, xs,
    back, home, sp, sp_recv, mids,
    in_sem, raw_sem, ag_s, ag_r, i_s, i_r, w_s, w_r, rs_s, rs_r, p_s, p_r, d_s, d_r, b_s, b_r, g_s, g_r, m_s, m_r,
):
    b = lax.axis_index("batch")
    h = lax.axis_index("head")
    p = b * HEADS + h
    mine = p // 16
    x, c = h // 2, h % 2
    sib = x * 2 + 1 - c

    def to_heads(src, dst, ssem, rsem):
        for i in range(1, HEADS):
            to = (h + i) % HEADS
            remote(src(to), dst.at[h], ssem, rsem, (b, to)).start()

    loads = [
        pltpu.make_async_copy(src, dst, in_sem.at[n])
        for n, (src, dst) in enumerate(
            [(wqk_hbm, wqk), (wvz_hbm, wvz), (states_hbm, states), (wo_hbm, wo), (sraw_hbm, sraw),
             (down_hbm, down), (wout_hbm, wout)]
        )
    ]
    wqk_in, wvz_in, states_in, wo_in, sraw_in, down_in, wout_in = loads
    for copy in loads:
        copy.start()

    def raw_in(n):
        return pltpu.make_async_copy(
            win_hbm.at[pl.ds(n * 8192, 8192)], raw.at[n % 2], raw_sem.at[n % 2]
        )

    raw_in(0).start()
    raw_in(1).start()

    barrier = pltpu.get_barrier_semaphore()

    @pl.loop(1, DEVS)
    def _(i):
        pl.semaphore_signal(barrier, inc=1, device_id=spot((p + i) % DEVS), device_id_type=MESH)

    wqk_in.wait()
    part_rows(wqk, wide, 2, lambda s: 128 * s, 8)
    pl.semaphore_wait(barrier, DEVS - 1)

    sent = []

    def pass_on(src, slot, to):
        copy = remote(src, hall.at[slot], ag_s.at[len(sent)], ag_r.at[slot], (b, to))
        copy.start()
        sent.append(copy)

    def norm_block(slot):
        rows = rms_scale(hall[slot].astype(F32).reshape(24, 2048), gain_in[...])
        nrm[pl.ds(pl.multiple_of(slot * 24, 8), 24)] = rows

    for d in (1, 3, 2):
        pass_on(hid_ref, h, ((x + d) % 4) * 2 + c)
    pass_on(hid_ref, h, sib)
    to_heads(lambda to: ids_ref, ids_all, i_s, i_r)
    to_heads(lambda to: wt_ref, wts_all, w_s, w_r)
    ids_all[h] = ids_ref[...]
    wts_all[h] = wt_ref[...]
    hall[h] = hid_ref[...]
    norm_block(h)
    wvz_in.wait()
    part_rows(wvz, wide, 4, lambda s: 256 + 128 * s, 16)
    for d in (3, 1, 2):
        slot = ((x + d) % 4) * 2 + c
        wait_bytes(hall.at[slot], ag_r.at[slot])
        pass_on(hall.at[slot], slot, sib)
    for d in (3, 1, 2):
        norm_block(((x + d) % 4) * 2 + c)
    for d in (0, 3, 1, 2):
        slot = ((x + d) % 4) * 2 + 1 - c
        wait_bytes(hall.at[slot], ag_r.at[slot])
        norm_block(slot)

    left = nrm[...].astype(BF16)
    for n in range(3):
        proj[:, 256 * n : 256 * n + 256] = mm(left, wide[:, 256 * n : 256 * n + 256])
    wba = wba_ref[...].astype(F32)
    wba = jnp.concatenate([wba[0], wba[1], jnp.zeros((4, 2048), F32)], axis=0).astype(BF16)
    bas[...] = lax.dot_general(left, wba, (((1,), (1,)), ((), ())), preferred_element_type=F32)

    states_in.wait()
    wo_in.wait()

    @pl.loop(0, HEADS)
    def _(i):
        o = (h + 1 + i) % HEADS
        at = pl.multiple_of(o * 24, 8)
        gated = delta_rows(
            proj[pl.ds(at, 24)], bas[pl.ds(at, 24)], rates_ref[...], gain_gate[...],
            states[pl.ds(pl.multiple_of(o * 8, 8), 8)],
        )
        gated = jnp.concatenate([gated, jnp.zeros((8, 256), F32)], axis=0).astype(BF16)
        partb[o] = mm(gated, wo[...])[:24].astype(BF16).reshape(3, 8, 2048)

        @pl.when(i < HEADS - 1)
        def _():
            remote(partb.at[o], rs.at[h], rs_s, rs_r, (b, o)).start()

    i0, i1 = iota((128, 128), 0), iota((128, 128), 1)
    later = one_hot((i0 // 32 == i1 // 32) & (i1 < i0)).astype(BF16)
    own = jnp.concatenate([ids_ref[...].reshape(24, 10), jnp.full((8, 10), -1, jnp.int32)], axis=0)
    own = jnp.concatenate([own] * 4, axis=0)
    col = iota((128, 256), 1)
    col_chunk, col_rank = (col // 4) % 4, (col % 2).astype(F32)
    named = (col // 16) * 2 + (col // 2) % 2
    row_chunk = iota((128, 256), 0) // 32

    @pl.loop(0, 8)
    def _(g):
        hot = count_hits(own, named + g * 32)
        before = mm(later, hot.astype(BF16))
        chosen = jnp.where((before == col_rank) & (row_chunk == col_chunk), hot, 0.0)
        placing[g] = chosen.T.astype(BF16)

    sraw_in.wait()
    part_rows(sraw, swin, 8, gate_up_lane, 4)

    take(rs, rs_r)
    total = partb[h].astype(F32)
    for i in range(1, HEADS):
        total = total + rs[(h + i) % HEADS].astype(F32)
    resid = (hid_ref[...].astype(F32) + total).astype(BF16)
    post = rms_scale(resid.astype(F32), gain_post[...].reshape(1, 1, 2048)).astype(BF16)
    rows = post.astype(F32).reshape(24, 2048)
    blank = jnp.zeros((8, 512), F32)
    stacked[...] = jnp.concatenate(
        [v for j in range(4) for v in (rows[:, 512 * j : 512 * j + 512], blank)], axis=0
    ).astype(BF16)
    for i in range(HEADS):
        psend[i, 0] = resid[:, :, 256 * i : 256 * i + 256]
        psend[i, 1] = post[:, :, 256 * i : 256 * i + 256]
    to_heads(lambda to: psend.at[to], slices, p_s, p_r)
    slices[h] = psend[h]

    @pl.loop(0, 8)
    def _(i):
        group = (mine + i) % 8
        rows = mm(placing[group], stacked[...]).astype(BF16)
        send[pl.ds(group * 16, 16)] = rows.reshape(16, 16, 512)
        spread(p, group * 16, send, recv, d_s, d_r.at[mine])

    take(slices, p_r)
    every = slices[:, 1].astype(F32).reshape(192, 256)
    up = mm(every.astype(BF16), swin[...])
    logit = jnp.sum(every * sgate_ref[...].astype(F32), axis=-1, keepdims=True)
    high = logit.astype(BF16).astype(F32)
    zero = jnp.zeros((192, 126), F32)
    sp[...] = (
        jnp.concatenate([up, high, logit - high, zero], axis=1).astype(BF16).reshape(HEADS, 3, 8, 1152)
    )
    to_heads(lambda to: sp.at[to], sp_recv, g_s, g_r)

    for n in range(4):
        raw_in(n).wait()
        part_rows(raw.at[n % 2], win, 8, gate_up_lane, 16, 0, n * 1024)
        if n < 2:
            raw_in(n + 2).start()

    take(ids_all, i_r)
    take(wts_all, w_r)
    ids = ids_all[...].reshape(192, 10)
    wts = wts_all[...].reshape(192, 10)
    i0, i1 = iota((192, 192), 0), iota((192, 192), 1)
    later2 = one_hot((i0 // 24 == i1 // 24) & (i1 < i0)).astype(BF16)
    col2 = iota((192, 512), 1)
    named2 = (col2 // 32) * 2 + (col2 // 16) % 2
    rank2 = ((col2 // 8) % 2).astype(F32)
    kept = iota((192, 512), 0) // 24 == col2 % 8

    @pl.loop(0, 8)
    def _(g):
        here = named2 + g * 32
        hot = jnp.zeros((192, 512), F32)
        heavy = jnp.zeros((192, 512), F32)
        for k in range(10):
            same = ids[:, k : k + 1] == here
            hot = hot + one_hot(same)
            heavy = heavy + jnp.where(same, wts[:, k : k + 1], 0.0)
        before = mm(later2, hot.astype(BF16))
        heavy = jnp.where((before == rank2) & kept, heavy, 0.0)
        top = heavy.astype(BF16)
        load[g, 0] = top
        load[g, 1] = (heavy - top.astype(F32)).astype(BF16)

    source, inside = iota((256, 256), 1) // 16, iota((256, 256), 1) % 16
    target = (inside // 4) * 64 + ((inside // 2) % 2) * 32 + (source // 8) * 16 + (inside % 2) * 8 + source % 8
    order = one_hot(iota((256, 256), 0) == target).astype(BF16)
    wout_in.wait()
    for half in range(2):
        @pl.loop(0, 4)
        def _(i):
            group = (mine + 8 - (4 * half + i)) % 8
            wait_bytes(recv.at[pl.ds(group * 16, 16)], d_r.at[group])
            got = mm(order, recv[pl.ds(group * 16, 16)].reshape(256, 512)).astype(BF16)
            to = pl.multiple_of(i * 32, 32)
            for j in range(4):
                for e in range(2):
                    at = j * 64 + e * 32
                    xs[e, pl.ds(to, 32), 512 * j : 512 * j + 512] = got[at : at + 32]

        @pl.loop(0, 2)
        def _(e):
            inner = []
            for n in range(2):
                lane = slice(256 * n, 256 * n + 256)
                lane2 = slice(512 + 256 * n, 768 + 256 * n)
                gate = mm(xs[e], win[pl.ds(e * 2048, 2048), lane])
                more = mm(xs[e], win[pl.ds(e * 2048, 2048), lane2])
                inner.append((silu(gate) * more).astype(BF16))
            inner = jnp.concatenate(inner, axis=1)
            rows = pl.ds(pl.multiple_of(e * 16, 16), 16)
            for f in range(HEADS):
                got = mm(inner, wout[e, :, 256 * f : 256 * f + 256]).astype(BF16)
                for i in range(4):
                    group = (mine + 8 - (4 * half + i)) % 8
                    for n in range(2):
                        at = 32 * i + 16 * n
                        back[group * 16 + n * 8 + f, rows, :] = got[at : at + 16]

        @pl.loop(0, 4)
        def _(i):
            group = (mine + 8 - (4 * half + i)) % 8
            spread(p, group * 16, back, home, b_s, b_r)

        if half == 0:
            take(sp_recv, g_r)
            total = sp[h].astype(F32)
            for i in range(1, HEADS):
                total = total + sp_recv[(h + i) % HEADS].astype(F32)
            logit = total[:, :, 1024:1025] + total[:, :, 1025:1026]
            mid = silu(total[:, :, :512]) * total[:, :, 512:1024] * jax.nn.sigmoid(logit)
            mids[h] = mid.astype(BF16)
            to_heads(lambda to: mids.at[h], mids, m_s, m_r)

    down_in.wait()
    take(mids, m_r)
    every = mids[...].astype(F32).reshape(192, 512).astype(BF16)
    shared = mm(every, down[...])
    near = slices[:, 0].astype(F32).reshape(192, 256) + shared
    wait_bytes(home, b_r)
    acc = jnp.zeros((192, 256), F32)
    for g in range(8):
        got = home[16 * g : 16 * g + 16].reshape(512, 256)
        acc = acc + mm(load[g, 0], got) + mm(load[g, 1], got)
    out = (near + acc.astype(BF16).astype(F32)).astype(BF16).reshape(HEADS, 3, 8, 256)
    for o in range(HEADS):
        out_ref[:, o] = out[o]
    for copy in sent:
        copy.wait_send()
    take(ids_all, i_s)
    take(wts_all, w_s)
    take(rs, rs_s)
    take(psend, p_s)
    take(send, d_s)
    take(sp, g_s)
    take(mids, m_s)
    take(back, b_s)


def layer(*args):
    dma = pltpu.SemaphoreType.DMA
    return pl.pallas_call(
        layer_kernel,
        name="layer",
        out_shape=jax.ShapeDtypeStruct((3, HEADS, 8, 256), BF16),
        in_specs=[VMEM] * 9 + [ANY] * 8,
        out_specs=VMEM,
        scratch_shapes=[
            pltpu.VMEM((HEADS, 3, 8, 2048), BF16),
            pltpu.VMEM((192, 2048), F32),
            pltpu.VMEM((192, 768), F32),
            pltpu.VMEM((192, 8), F32),
            pltpu.VMEM((64, 2, 128, 128), F32),
            pltpu.VMEM((4096, 128), BF16),
            pltpu.VMEM((8192, 128), BF16),
            pltpu.VMEM((2048, 768), BF16),
            pltpu.VMEM((256, 2048), BF16),
            pltpu.VMEM((2048, 128), BF16),
            pltpu.VMEM((256, 1024), BF16),
            pltpu.VMEM((512, 256), BF16),
            pltpu.VMEM((2, 8192, 128), BF16),
            pltpu.VMEM((4096, 1024), BF16),
            pltpu.VMEM((2, 512, 2048), BF16),
            pltpu.VMEM((HEADS, 3, 8, 10), jnp.int32),
            pltpu.VMEM((HEADS, 3, 8, 10), F32),
            pltpu.VMEM((HEADS, 3, 8, 2048), BF16),
            pltpu.VMEM((HEADS, 3, 8, 2048), BF16),
            pltpu.VMEM((DEVS, 16, 512), BF16),
            pltpu.VMEM((DEVS, 16, 512), BF16),
            pltpu.VMEM((HEADS, 2, 3, 8, 256), BF16),
            pltpu.VMEM((HEADS, 2, 3, 8, 256), BF16),
            pltpu.VMEM((128, 512), BF16),
            pltpu.VMEM((8, 256, 128), BF16),
            pltpu.VMEM((8, 2, 192, 512), BF16),
            pltpu.VMEM((2, 128, 2048), BF16),
            pltpu.VMEM((DEVS, 32, 256), BF16),
            pltpu.VMEM((DEVS, 32, 256), BF16),
            pltpu.VMEM((HEADS, 3, 8, 1152), BF16),
            pltpu.VMEM((HEADS, 3, 8, 1152), BF16),
            pltpu.VMEM((HEADS, 3, 8, 512), BF16),
            dma((7,)), dma((2,)), dma((7,)), dma((HEADS,)),
        ]
        + [dma(())] * 9
        + [dma((8,))]
        + [dma(())] * 6,
        compiler_params=pltpu.CompilerParams(
            collective_id=0, has_side_effects=True, vmem_limit_bytes=60 * 2**20
        ),
    )(*args)


def column_rows(w):
    return w.reshape(-1, 2, 4, 128).transpose(0, 2, 1, 3).reshape(-1, 128)


def shards(
    hidden_in, states, norm_in, w_qk, w_vz, w_ba, a_log, dt_bias, norm_gate, w_out, norm_post,
    shared_in, shared_gate, shared_out, expert_in, expert_out, routes, route_weight,
):
    out = layer(
        hidden_in.transpose(1, 0, 2),
        routes.transpose(1, 0, 2),
        route_weight.transpose(1, 0, 2),
        norm_in.reshape(1, 2048),
        jnp.stack([a_log, dt_bias]),
        norm_gate.reshape(1, 128),
        norm_post.reshape(1, 2048),
        w_ba.transpose(1, 2, 0),
        shared_gate.reshape(1, 256),
        states,
        w_qk.reshape(4096, 128),
        w_vz.reshape(8192, 128),
        w_out.reshape(256, 2048),
        column_rows(shared_in),
        shared_out,
        column_rows(expert_in),
        expert_out,
    )
    return out.reshape(3, 64, 256).transpose(1, 0, 2)


def solution(mesh):
    in_specs = (
        P(("batch", "head"), None, None),
        P("batch", "head", None, None),
        P(),
        P(None, "head", None, None),
        P(None, "head", None, None),
        P(None, None, "head"),
        P("head"),
        P("head"),
        P(),
        P("head", None, None),
        P(),
        P("head", None, None),
        P("head"),
        P(None, "head"),
        P(("batch", "head"), None, None, None),
        P(("batch", "head"), None, None),
        P(("batch", "head"), None, None),
        P(("batch", "head"), None, None),
    )
    out_specs = P("batch", None, "head")
    return jax.shard_map(shards, mesh=mesh, in_specs=in_specs, out_specs=out_specs, check_vma=False)
```

```python
import jax
import jax.numpy as jnp
from jax import lax
from jax.experimental import pallas as pl
from jax.experimental.pallas import tpu as pltpu
from jax.sharding import PartitionSpec as P

EPS = 1e-06
MESH = pl.DeviceIdType.MESH
HEADS = 8
BATCH = 16
DEVS = HEADS * BATCH
F32 = jnp.float32
BF16 = jnp.bfloat16
VMEM = pl.BlockSpec(memory_space=pltpu.VMEM)
ANY = pl.BlockSpec(memory_space=pl.ANY)


def rms_scale(values, gain):
    return values * lax.rsqrt(jnp.mean(values * values, axis=-1, keepdims=True) + EPS) * gain


def unit_norm(v):
    return v * lax.rsqrt(jnp.sum(v * v, axis=-1, keepdims=True) + EPS)


def silu(v):
    return v * jax.nn.sigmoid(v)


def iota(shape, axis):
    return lax.broadcasted_iota(jnp.int32, shape, axis)


def mm(left, right):
    return jnp.dot(left, right, preferred_element_type=F32)


def one_hot(mask):
    return jnp.where(mask, 1.0, 0.0)


def spot(p):
    return (p // HEADS, p % HEADS)


def remote(src, dst, send_sem, recv_sem, to):
    return pltpu.make_async_remote_copy(
        src_ref=src, dst_ref=dst, send_sem=send_sem, recv_sem=recv_sem, device_id=to, device_id_type=MESH
    )


def wait_bytes(ref, sem):
    pltpu.make_async_copy(ref, ref, sem).wait()


def take(ref, sem):
    wait_bytes(ref.at[pl.ds(0, ref.shape[0] - 1)], sem)


def plane_offset(place):
    dy = (place % 8) // 2
    return dy, (place % 2) * 2 + (dy + place // 8) % 2


def far_first(half):
    def hops(position):
        dy, dz = plane_offset(position // 8)
        return sum(min(d, 4 - d) for d in (dy, dz, (position % 8) // 2))

    return sorted(range(64 * half, 64 * half + 64), key=lambda position: (-hops(position), position % 5, position))


def part_rows(raw, wide, kinds, lane_of, blocks, from_row=0, to_row=0):
    count = 256 // kinds
    order = one_hot(iota((256, 256), 1) == (iota((256, 256), 0) % count) * kinds + iota((256, 256), 0) // count)
    order = order.astype(BF16)

    @pl.loop(0, blocks, unroll=4)
    def _(i):
        at = pl.multiple_of(from_row + i * 512, 512)
        to = pl.multiple_of(to_row + i * 2 * count, 2 * count)
        pair = jnp.concatenate([raw[pl.ds(at, 256)], raw[pl.ds(at + 256, 256)]], axis=1)
        got = mm(order, pair).astype(BF16)
        for s in range(kinds):
            lane = lane_of(s)
            part = got[count * s : count * s + count]
            wide[pl.ds(to, count), lane : lane + 128] = part[:, :128]
            wide[pl.ds(to + count, count), lane : lane + 128] = part[:, 128:]


def gate_up_lane(s):
    return (s % 2) * 512 + (s // 2) * 128


def count_hits(ids, here):
    hot = jnp.zeros(here.shape, F32)
    for k in range(10):
        hot = hot + one_hot(ids[:, k : k + 1] == here)
    return hot


def delta_rows(rows, ba, rates, gain, states):
    q = unit_norm(silu(rows[:, :128])) * (128 ** -0.5)
    k = unit_norm(silu(rows[:, 128:256]))
    left = jnp.concatenate([k, q], axis=0)
    place = iota((48, 128), 0) % 8
    left = jnp.concatenate([jnp.where(place == s, left, 0.0) for s in range(8)], axis=1)
    right = jnp.concatenate(
        [states[:, 0].reshape(1024, 128), states[:, 1].reshape(1024, 128)], axis=1
    ).astype(BF16)
    met = mm(left.astype(BF16), right)
    q = [q[8 * t : 8 * t + 8] for t in range(3)]
    k = [k[8 * t : 8 * t + 8] for t in range(3)]

    def along(u, v):
        return jnp.sum(u * v, axis=-1, keepdims=True)

    kk = {(i, t): along(k[i], k[t]) for i in range(3) for t in range(i + 1, 3)}
    kq = {(i, t): along(k[i], q[t]) for i in range(3) for t in range(i, 3)}
    heads = []
    for j in range(2):
        lane = slice(128 * j, 128 * j + 128)
        values = silu(rows[:, 256 + 256 * j : 384 + 256 * j])
        gate_z = silu(rows[:, 384 + 256 * j : 512 + 256 * j])
        raw = ba[:, 2 + j : 3 + j] + rates[1][:, j : j + 1]
        decays = jnp.exp(-jnp.exp(rates[0][:, j : j + 1]) * jax.nn.softplus(raw))
        betas = jax.nn.sigmoid(ba[:, j : j + 1])
        decay = [decays[8 * t : 8 * t + 8] for t in range(3)]
        deltas, steps = [], []
        for t in range(3):
            whole = decay[0]
            for i in range(1, t + 1):
                whole = whole * decay[i]
            recalled = whole * met[8 * t : 8 * t + 8, lane]
            readout = whole * met[24 + 8 * t : 32 + 8 * t, lane]
            fade = jnp.ones_like(whole)
            for i in range(t - 1, -1, -1):
                fade = fade * decay[i + 1]
                recalled = recalled + (fade * kk[i, t]) * deltas[i]
                readout = readout + (fade * kq[i, t]) * deltas[i]
            deltas.append(betas[8 * t : 8 * t + 8] * (values[8 * t : 8 * t + 8] - recalled))
            readout = readout + kq[t, t] * deltas[t]
            steps.append(rms_scale(readout, gain) * gate_z[8 * t : 8 * t + 8])
        heads.append(jnp.concatenate(steps, axis=0))
    return jnp.concatenate(heads, axis=1)


def layer_kernel(
    hid_ref, ids_ref, wt_ref, gain_in, alog_ref, dt_ref, gain_gate, gain_post, wba_ref, sgate_ref,
    states_hbm, wqk_hbm, wvz_hbm, wo_hbm, sraw_hbm, down_hbm, win_hbm, wout_hbm,
    out_ref,
    hall, nrm, proj, bas, states, wqk, wvz, wide, wo, sraw, swin, down, raw, win, wout,
    ids_all, wts_all, partb, fs, rs, send, recv, psend, slices, stacked, placing, load, xs,
    back, home, sp, sp_recv, mids,
    in_sem, raw_sem, ag_s, ag_r, i_s, i_r, w_s, w_r, f_s, f_r, rs_s, rs_r, p_s, p_r, d_s, d_r, b_s, b_r, g_s, g_r, m_s, m_r,
):
    b = lax.axis_index("batch")
    h = lax.axis_index("head")
    p = b * HEADS + h
    x, c = h // 2, h % 2
    sib = x * 2 + 1 - c
    y, z = b // 4, b % 4

    def batch_at(place, sign):
        dy, dz = plane_offset(place)
        return ((y + 4 + sign * dy) % 4) * 4 + (z + 4 + sign * dz) % 4

    def head_at(member, sign):
        return ((x + 4 + sign * (member // 2)) % 4) * 2 + (c + member) % 2

    def to_heads(src, dst, ssem, rsem):
        for i in range(1, HEADS):
            to = (h + i) % HEADS
            remote(src(to), dst.at[h], ssem, rsem, (b, to)).start()

    pairs = [
        (wqk_hbm, wqk), (wvz_hbm, wvz), (sraw_hbm, sraw), (states_hbm, states), (wo_hbm, wo),
        (down_hbm, down), (wout_hbm, wout),
    ]
    loads = [pltpu.make_async_copy(src, dst, in_sem.at[n]) for n, (src, dst) in enumerate(pairs)]
    wqk_in, wvz_in, sraw_in, states_in, wo_in, down_in, wout_in = loads

    def raw_in(n):
        return pltpu.make_async_copy(
            win_hbm.at[pl.ds(n * 8192, 8192)], raw.at[n % 2], raw_sem.at[n % 2]
        )

    for copy in loads[:4]:
        copy.start()
    raw_in(0).start()
    raw_in(1).start()
    for copy in loads[4:]:
        copy.start()

    barrier = pltpu.get_barrier_semaphore()

    @pl.loop(1, DEVS)
    def _(i):
        pl.semaphore_signal(barrier, inc=1, device_id=spot((p + i) % DEVS), device_id_type=MESH)

    pl.semaphore_wait(barrier, DEVS - 1)

    sent = []

    def pass_on(src, slot, to):
        copy = remote(src, hall.at[slot], ag_s.at[len(sent)], ag_r.at[slot], (b, to))
        copy.start()
        sent.append(copy)

    def norm_block(slot):
        rows = rms_scale(hall[slot].astype(F32).reshape(24, 2048), gain_in[...])
        nrm[pl.ds(pl.multiple_of(slot * 24, 8), 24)] = rows

    for d in (2, 1, 3):
        pass_on(hid_ref, h, ((x + d) % 4) * 2 + c)
    pass_on(hid_ref, h, sib)
    to_heads(lambda to: ids_ref, ids_all, i_s, i_r)
    to_heads(lambda to: wt_ref, wts_all, w_s, w_r)
    ids_all[h] = ids_ref[...]
    wts_all[h] = wt_ref[...]
    hall[h] = hid_ref[...]
    norm_block(h)
    wqk_in.wait()
    part_rows(wqk, wide, 2, lambda s: 128 * s, 8)

    def forward(d):
        slot = ((x + d) % 4) * 2 + c
        wait_bytes(hall.at[slot], ag_r.at[slot])
        pass_on(hall.at[slot], slot, sib)

    forward(3)
    forward(1)
    forward(2)
    wvz_in.wait()
    part_rows(wvz, wide, 4, lambda s: 256 + 128 * s, 16)
    for d in (3, 1, 2):
        norm_block(((x + d) % 4) * 2 + c)
    for d in (0, 3, 1, 2):
        slot = ((x + d) % 4) * 2 + 1 - c
        wait_bytes(hall.at[slot], ag_r.at[slot])
        norm_block(slot)

    left = nrm[...].astype(BF16)
    for n in range(3):
        proj[:, 256 * n : 256 * n + 256] = mm(left, wide[:, 256 * n : 256 * n + 256])
    wba = wba_ref[...].astype(F32)
    wba = jnp.concatenate([wba[0], wba[1], jnp.zeros((4, 2048), F32)], axis=0).astype(BF16)
    bas[...] = lax.dot_general(left, wba, (((1,), (1,)), ((), ())), preferred_element_type=F32)

    states_in.wait()
    wo_in.wait()

    def partial_rows(o):
        at = pl.multiple_of(o * 24, 8)
        gated = delta_rows(
            proj[pl.ds(at, 24)], bas[pl.ds(at, 24)], (alog_ref[...], dt_ref[...]), gain_gate[...],
            states[pl.ds(pl.multiple_of(o * 8, 8), 8)],
        )
        gated = jnp.concatenate([gated, jnp.zeros((8, 256), F32)], axis=0).astype(BF16)
        return mm(gated, wo[...])[:24].reshape(3, 8, 2048)

    @pl.loop(0, 3)
    def _(k):
        o = ((x + 1 + k) % 4) * 2 + 1 - c
        partb[o] = partial_rows(o).astype(BF16)
        remote(partb.at[o], fs.at[k], f_s, f_r.at[k], (b, sib)).start()

    @pl.loop(0, 3)
    def _(k):
        o = ((x + 1 + k) % 4) * 2 + c
        rows = partial_rows(o)
        wait_bytes(fs.at[k], f_r.at[k])
        partb[o] = (rows + fs[k].astype(F32)).astype(BF16)
        remote(partb.at[o], rs.at[k], rs_s, rs_r, (b, o)).start()

    partb[sib] = partial_rows(sib).astype(BF16)
    remote(partb.at[sib], rs.at[3], rs_s, rs_r, (b, sib)).start()
    total = partial_rows(h)

    i0, i1 = iota((128, 128), 0), iota((128, 128), 1)
    later = one_hot((i0 // 32 == i1 // 32) & (i1 < i0)).astype(BF16)
    own = jnp.concatenate([ids_ref[...].reshape(24, 10), jnp.full((8, 10), -1, jnp.int32)], axis=0)
    own = jnp.concatenate([own] * 4, axis=0)
    col = iota((128, 256), 1)
    col_chunk, col_rank = (col // 4) % 4, (col % 2).astype(F32)
    named = head_at((col // 16) % 8, 1) * 2 + (col // 2) % 2
    row_chunk = iota((128, 256), 0) // 32

    @pl.loop(0, 8)
    def _(g):
        first, second = batch_at(2 * g, 1) * 16, batch_at(2 * g + 1, 1) * 16
        hot = count_hits(own, named + jnp.where(col < 128, first, second))
        before = mm(later, hot.astype(BF16))
        chosen = jnp.where((before == col_rank) & (row_chunk == col_chunk), hot, 0.0)
        placing[g] = chosen.T.astype(BF16)

    sraw_in.wait()
    part_rows(sraw, swin, 8, gate_up_lane, 4)

    wait_bytes(rs, rs_r)
    for i in range(4):
        total = total + rs[i].astype(F32)
    resid = (hid_ref[...].astype(F32) + total).astype(BF16)
    post = rms_scale(resid.astype(F32), gain_post[...].reshape(1, 1, 2048)).astype(BF16)
    rows = post.astype(F32).reshape(24, 2048)
    blank = jnp.zeros((8, 512), F32)
    stacked[...] = jnp.concatenate(
        [v for j in range(4) for v in (rows[:, 512 * j : 512 * j + 512], blank)], axis=0
    ).astype(BF16)
    for i in range(HEADS):
        psend[i, 0] = resid[:, :, 256 * i : 256 * i + 256]
        psend[i, 1] = post[:, :, 256 * i : 256 * i + 256]
    to_heads(lambda to: psend.at[to], slices, p_s, p_r)
    slices[h] = psend[h]

    for half in range(2):
        @pl.loop(4 * half, 4 * half + 4)
        def _(g):
            rows = mm(placing[g], stacked[...]).astype(BF16)
            send[pl.ds(g * 16, 16)] = rows.reshape(16, 16, 512)

        for n in far_first(half):
            if n:
                to = (batch_at(n // 8, 1), head_at(n % 8, 1))
                remote(send.at[n], recv.at[n], d_s, d_r.at[half], to).start()
            else:
                pltpu.make_async_copy(send.at[n], recv.at[n], d_r.at[half]).start()

    def lay_out(n):
        raw_in(n).wait()
        part_rows(raw.at[n % 2], win, 8, gate_up_lane, 16, 0, n * 1024)
        if n < 2:
            raw_in(n + 2).start()

    lay_out(0)
    lay_out(1)
    take(slices, p_r)
    every = slices[:, 1].astype(F32).reshape(192, 256)
    up = mm(every.astype(BF16), swin[...])
    logit = jnp.sum(every * sgate_ref[...].astype(F32), axis=-1, keepdims=True)
    high = logit.astype(BF16).astype(F32)
    zero = jnp.zeros((192, 126), F32)
    sp[...] = (
        jnp.concatenate([up, high, logit - high, zero], axis=1).astype(BF16).reshape(HEADS, 3, 8, 1152)
    )
    to_heads(lambda to: sp.at[to], sp_recv, g_s, g_r)

    lay_out(2)
    lay_out(3)

    take(ids_all, i_r)
    take(wts_all, w_r)
    ids = ids_all[...].reshape(192, 10)
    wts = wts_all[...].reshape(192, 10)
    i0, i1 = iota((192, 192), 0), iota((192, 192), 1)
    later2 = one_hot((i0 // 24 == i1 // 24) & (i1 < i0)).astype(BF16)
    named2 = iota((192, 64), 1) // 2
    rank2 = (iota((192, 64), 1) % 2).astype(F32)
    widen = one_hot(iota((64, 512), 1) // 8 == iota((64, 512), 0)).astype(BF16)
    col2 = iota((384, 512), 1)
    source_head, member = (col2 // 32) % 8, col2 % 8
    owner = ((source_head // 2 + 4 - member // 2) % 4) * 2 + (source_head + member) % 2
    kept = (iota((384, 512), 0) % 192) // 24 == owner

    @pl.loop(0, 8)
    def _(g):
        here = named2 + g * 32
        hot = jnp.zeros((192, 64), F32)
        heavy = jnp.zeros((192, 64), F32)
        for k in range(10):
            same = ids[:, k : k + 1] == here
            hot = hot + one_hot(same)
            heavy = heavy + jnp.where(same, wts[:, k : k + 1], 0.0)
        before = mm(later2, hot.astype(BF16))
        heavy = jnp.where(before == rank2, heavy, 0.0)
        top = heavy.astype(BF16)
        both = jnp.concatenate([top, (heavy - top.astype(F32)).astype(BF16)], axis=0)
        load[g] = jnp.where(kept, mm(both, widen), 0.0).astype(BF16)

    source, inside = iota((256, 256), 1) // 16, iota((256, 256), 1) % 16
    target = (inside // 4) * 64 + ((inside // 2) % 2) * 32 + (source // 8) * 16 + (inside % 2) * 8 + source % 8
    order = one_hot(iota((256, 256), 0) == target).astype(BF16)
    wout_in.wait()
    for half in range(2):
        wait_bytes(recv.at[pl.ds(64 * half, 64)], d_r.at[half])

        @pl.loop(0, 4)
        def _(i):
            got = mm(order, recv[pl.ds(64 * half + i * 16, 16)].reshape(256, 512)).astype(BF16)
            to = pl.multiple_of(i * 32, 32)
            for j in range(4):
                for e in range(2):
                    at = j * 64 + e * 32
                    xs[e, pl.ds(to, 32), 512 * j : 512 * j + 512] = got[at : at + 32]

        @pl.loop(0, 2)
        def _(e):
            inner = []
            for n in range(2):
                lane = slice(256 * n, 256 * n + 256)
                lane2 = slice(512 + 256 * n, 768 + 256 * n)
                gate = mm(xs[e], win[pl.ds(e * 2048, 2048), lane])
                more = mm(xs[e], win[pl.ds(e * 2048, 2048), lane2])
                inner.append((silu(gate) * more).astype(BF16))
            inner = jnp.concatenate(inner, axis=1)
            rows = pl.ds(pl.multiple_of(e * 16, 16), 16)
            for f in range(HEADS):
                got = mm(inner, wout[e, :, 256 * f : 256 * f + 256]).astype(BF16)
                for i in range(8):
                    back[64 * half + 8 * i + f, rows, :] = got[16 * i : 16 * i + 16]

        for n in far_first(half):
            batch, f = batch_at(n // 8, -1), head_at(n % 8, -1)
            if n:
                remote(back.at[n // 8 * 8 + f], home.at[p], b_s, b_r, (batch, f)).start()
            else:
                pltpu.make_async_copy(back.at[f], home.at[p], b_r).start()

        if half == 0:
            take(sp_recv, g_r)
            total = sp[h].astype(F32)
            for i in range(1, HEADS):
                total = total + sp_recv[(h + i) % HEADS].astype(F32)
            logit = total[:, :, 1024:1025] + total[:, :, 1025:1026]
            mid = silu(total[:, :, :512]) * total[:, :, 512:1024] * jax.nn.sigmoid(logit)
            mids[h] = mid.astype(BF16)
            to_heads(lambda to: mids.at[h], mids, m_s, m_r)

    down_in.wait()
    take(mids, m_r)
    every = mids[...].astype(F32).reshape(192, 512).astype(BF16)
    shared = mm(every, down[...])
    near = slices[:, 0].astype(F32).reshape(192, 256) + shared
    wait_bytes(home, b_r)
    acc = jnp.zeros((384, 256), F32)
    for g in range(8):
        acc = acc + mm(load[g], home[16 * g : 16 * g + 16].reshape(512, 256))
    acc = acc[:192] + acc[192:]
    out = (near + acc.astype(BF16).astype(F32)).astype(BF16).reshape(HEADS, 3, 8, 256)
    for o in range(HEADS):
        out_ref[:, o] = out[o]
    for copy in sent:
        copy.wait_send()
    take(ids_all, i_s)
    take(wts_all, w_s)
    wait_bytes(fs, f_s)
    wait_bytes(rs, rs_s)
    take(psend, p_s)
    take(send, d_s)
    take(sp, g_s)
    take(mids, m_s)
    take(back, b_s)


def layer(*args):
    dma = pltpu.SemaphoreType.DMA
    return pl.pallas_call(
        layer_kernel,
        name="layer",
        out_shape=jax.ShapeDtypeStruct((3, HEADS, 8, 256), BF16),
        in_specs=[VMEM] * 10 + [ANY] * 8,
        out_specs=VMEM,
        scratch_shapes=[
            pltpu.VMEM((HEADS, 3, 8, 2048), BF16),
            pltpu.VMEM((192, 2048), F32),
            pltpu.VMEM((192, 768), F32),
            pltpu.VMEM((192, 8), F32),
            pltpu.VMEM((64, 2, 128, 128), F32),
            pltpu.VMEM((4096, 128), BF16),
            pltpu.VMEM((8192, 128), BF16),
            pltpu.VMEM((2048, 768), BF16),
            pltpu.VMEM((256, 2048), BF16),
            pltpu.VMEM((2048, 128), BF16),
            pltpu.VMEM((256, 1024), BF16),
            pltpu.VMEM((512, 256), BF16),
            pltpu.VMEM((2, 8192, 128), BF16),
            pltpu.VMEM((4096, 1024), BF16),
            pltpu.VMEM((2, 512, 2048), BF16),
            pltpu.VMEM((HEADS, 3, 8, 10), jnp.int32),
            pltpu.VMEM((HEADS, 3, 8, 10), F32),
            pltpu.VMEM((HEADS, 3, 8, 2048), BF16),
            pltpu.VMEM((3, 3, 8, 2048), BF16),
            pltpu.VMEM((4, 3, 8, 2048), BF16),
            pltpu.VMEM((DEVS, 16, 512), BF16),
            pltpu.VMEM((DEVS, 16, 512), BF16),
            pltpu.VMEM((HEADS, 2, 3, 8, 256), BF16),
            pltpu.VMEM((HEADS, 2, 3, 8, 256), BF16),
            pltpu.VMEM((128, 512), BF16),
            pltpu.VMEM((8, 256, 128), BF16),
            pltpu.VMEM((8, 384, 512), BF16),
            pltpu.VMEM((2, 128, 2048), BF16),
            pltpu.VMEM((DEVS, 32, 256), BF16),
            pltpu.VMEM((DEVS, 32, 256), BF16),
            pltpu.VMEM((HEADS, 3, 8, 1152), BF16),
            pltpu.VMEM((HEADS, 3, 8, 1152), BF16),
            pltpu.VMEM((HEADS, 3, 8, 512), BF16),
            dma((7,)), dma((2,)), dma((7,)), dma((HEADS,)),
        ]
        + [dma(())] * 5
        + [dma((3,))]
        + [dma(())] * 5
        + [dma((2,))]
        + [dma(())] * 6,
        compiler_params=pltpu.CompilerParams(
            collective_id=0, has_side_effects=True, vmem_limit_bytes=60 * 2**20
        ),
    )(*args)


def column_rows(w):
    return w.reshape(-1, 2, 4, 128).transpose(0, 2, 1, 3).reshape(-1, 128)


def shards(
    hidden_in, states, norm_in, w_qk, w_vz, w_ba, a_log, dt_bias, norm_gate, w_out, norm_post,
    shared_in, shared_gate, shared_out, expert_in, expert_out, routes, route_weight,
):
    out = layer(
        hidden_in.transpose(1, 0, 2),
        routes.transpose(1, 0, 2),
        route_weight.transpose(1, 0, 2),
        norm_in.reshape(1, 2048),
        a_log.reshape(1, 2),
        dt_bias.reshape(1, 2),
        norm_gate.reshape(1, 128),
        norm_post.reshape(1, 2048),
        w_ba.transpose(1, 2, 0),
        shared_gate.reshape(1, 256),
        states,
        w_qk.reshape(4096, 128),
        w_vz.reshape(8192, 128),
        w_out.reshape(256, 2048),
        column_rows(shared_in),
        shared_out,
        column_rows(expert_in),
        expert_out,
    )
    return out.reshape(3, 64, 256).transpose(1, 0, 2)


def solution(mesh):
    in_specs = (
        P(("batch", "head"), None, None),
        P("batch", "head", None, None),
        P(),
        P(None, "head", None, None),
        P(None, "head", None, None),
        P(None, None, "head"),
        P("head"),
        P("head"),
        P(),
        P("head", None, None),
        P(),
        P("head", None, None),
        P("head"),
        P(None, "head"),
        P(("batch", "head"), None, None, None),
        P(("batch", "head"), None, None),
        P(("batch", "head"), None, None),
        P(("batch", "head"), None, None),
    )
    out_specs = P("batch", None, "head")
    return jax.shard_map(shards, mesh=mesh, in_specs=in_specs, out_specs=out_specs, check_vma=False)
```

```python
import jax
import jax.numpy as jnp
from jax import lax
from jax.experimental import pallas as pl
from jax.experimental.pallas import tpu as pltpu
from jax.sharding import PartitionSpec as P

EPS = 1e-06
MESH = pl.DeviceIdType.MESH
HEADS = 8
BATCH = 16
DEVS = HEADS * BATCH
CUTS = (0, 64, 128)
PARTS = len(CUTS) - 1
F32 = jnp.float32
BF16 = jnp.bfloat16
VMEM = pl.BlockSpec(memory_space=pltpu.VMEM)
ANY = pl.BlockSpec(memory_space=pl.ANY)


def rms_scale(values, gain):
    return values * lax.rsqrt(jnp.mean(values * values, axis=-1, keepdims=True) + EPS) * gain


def unit_norm(v):
    return v * lax.rsqrt(jnp.sum(v * v, axis=-1, keepdims=True) + EPS)


def silu(v):
    return v * jax.nn.sigmoid(v)


def iota(shape, axis):
    return lax.broadcasted_iota(jnp.int32, shape, axis)


def mm(left, right):
    return jnp.dot(left, right, preferred_element_type=F32)


def one_hot(mask):
    return jnp.where(mask, 1.0, 0.0)


def spot(p):
    return (p // HEADS, p % HEADS)


def remote(src, dst, send_sem, recv_sem, to):
    return pltpu.make_async_remote_copy(
        src_ref=src, dst_ref=dst, send_sem=send_sem, recv_sem=recv_sem, device_id=to, device_id_type=MESH
    )


def wait_bytes(ref, sem):
    pltpu.make_async_copy(ref, ref, sem).wait()


def take(ref, sem):
    wait_bytes(ref.at[pl.ds(0, ref.shape[0] - 1)], sem)


def plane_offset(place):
    dy = (place % 8) // 2
    return dy, (place % 2) * 2 + (dy + place // 8) % 2


def far_first(part):
    def hops(position):
        dy, dz = plane_offset(position // 8)
        return sum(min(d, 4 - d) for d in (dy, dz, (position % 8) // 2))

    return sorted(range(CUTS[part], CUTS[part + 1]), key=lambda position: (-hops(position), position % 5, position))


def part_rows(raw, wide, kinds, lane_of, blocks, from_row=0, to_row=0):
    count = 256 // kinds
    order = one_hot(iota((256, 256), 1) == (iota((256, 256), 0) % count) * kinds + iota((256, 256), 0) // count)
    order = order.astype(BF16)

    @pl.loop(0, blocks, unroll=4)
    def _(i):
        at = pl.multiple_of(from_row + i * 512, 512)
        to = pl.multiple_of(to_row + i * 2 * count, 2 * count)
        pair = jnp.concatenate([raw[pl.ds(at, 256)], raw[pl.ds(at + 256, 256)]], axis=1)
        got = mm(order, pair).astype(BF16)
        for s in range(kinds):
            lane = lane_of(s)
            part = got[count * s : count * s + count]
            wide[pl.ds(to, count), lane : lane + 128] = part[:, :128]
            wide[pl.ds(to + count, count), lane : lane + 128] = part[:, 128:]


def gate_up_lane(s):
    return (s % 2) * 512 + (s // 2) * 128


def count_hits(ids, here):
    hot = jnp.zeros(here.shape, F32)
    for k in range(10):
        hot = hot + one_hot(ids[:, k : k + 1] == here)
    return hot


def delta_rows(rows, ba, rates, gain, states):
    q = unit_norm(silu(rows[:, :128])) * (128 ** -0.5)
    k = unit_norm(silu(rows[:, 128:256]))
    left = jnp.concatenate([k, q], axis=0)
    place = iota((48, 128), 0) % 8
    left = jnp.concatenate([jnp.where(place == s, left, 0.0) for s in range(8)], axis=1)
    right = jnp.concatenate(
        [states[:, 0].reshape(1024, 128), states[:, 1].reshape(1024, 128)], axis=1
    ).astype(BF16)
    met = mm(left.astype(BF16), right)
    q = [q[8 * t : 8 * t + 8] for t in range(3)]
    k = [k[8 * t : 8 * t + 8] for t in range(3)]

    def along(u, v):
        return jnp.sum(u * v, axis=-1, keepdims=True)

    kk = {(i, t): along(k[i], k[t]) for i in range(3) for t in range(i + 1, 3)}
    kq = {(i, t): along(k[i], q[t]) for i in range(3) for t in range(i, 3)}
    heads = []
    for j in range(2):
        lane = slice(128 * j, 128 * j + 128)
        values = silu(rows[:, 256 + 256 * j : 384 + 256 * j])
        gate_z = silu(rows[:, 384 + 256 * j : 512 + 256 * j])
        raw = ba[:, 2 + j : 3 + j] + rates[1][:, j : j + 1]
        decays = jnp.exp(-jnp.exp(rates[0][:, j : j + 1]) * jax.nn.softplus(raw))
        betas = jax.nn.sigmoid(ba[:, j : j + 1])
        decay = [decays[8 * t : 8 * t + 8] for t in range(3)]
        deltas, steps = [], []
        for t in range(3):
            whole = decay[0]
            for i in range(1, t + 1):
                whole = whole * decay[i]
            recalled = whole * met[8 * t : 8 * t + 8, lane]
            readout = whole * met[24 + 8 * t : 32 + 8 * t, lane]
            fade = jnp.ones_like(whole)
            for i in range(t - 1, -1, -1):
                fade = fade * decay[i + 1]
                recalled = recalled + (fade * kk[i, t]) * deltas[i]
                readout = readout + (fade * kq[i, t]) * deltas[i]
            deltas.append(betas[8 * t : 8 * t + 8] * (values[8 * t : 8 * t + 8] - recalled))
            readout = readout + kq[t, t] * deltas[t]
            steps.append(rms_scale(readout, gain) * gate_z[8 * t : 8 * t + 8])
        heads.append(jnp.concatenate(steps, axis=0))
    return jnp.concatenate(heads, axis=1)


def layer_kernel(
    hid_hbm, ids_hbm, wt_hbm, gain_in_hbm, alog_hbm, dt_hbm, gain_gate_hbm, gain_post_hbm, wba_hbm, sgate_hbm,
    states_hbm, wqk_hbm, wvz_hbm, wo_hbm, sraw_hbm, down_hbm, win_hbm, wout_hbm,
    out_ref,
    hid_ref, ids_ref, wt_ref, gain_in, alog_ref, dt_ref, gain_gate, gain_post, wba_ref, sgate_ref, hall, nrm, proj, bas, states, wqk, wvz, wide, wo, sraw, swin, down, raw, win, wout,
    ids_all, wts_all, partb, fs, rs, send, recv, psend, slices, stacked, placing, load, xs,
    back, home, sp, sp_recv, mids,
    small_sem, in_sem, raw_sem, ag_s, ag_r, i_s, i_r, w_s, w_r, f_s, f_r, rs_s, rs_r, p_s, p_r, d_s, d_r, b_s, b_r, g_s, g_r, m_s, m_r,
):
    b = lax.axis_index("batch")
    h = lax.axis_index("head")
    p = b * HEADS + h
    x, c = h // 2, h % 2
    sib = x * 2 + 1 - c
    y, z = b // 4, b % 4

    def batch_at(place, sign):
        dy, dz = plane_offset(place)
        return ((y + 4 + sign * dy) % 4) * 4 + (z + 4 + sign * dz) % 4

    def head_at(member, sign):
        return ((x + 4 + sign * (member // 2)) % 4) * 2 + (c + member) % 2

    def to_heads(src, dst, ssem, rsem):
        for i in range(1, HEADS):
            to = (h + i) % HEADS
            remote(src(to), dst.at[h], ssem, rsem, (b, to)).start()

    pairs = [
        (wqk_hbm, wqk), (wvz_hbm, wvz), (sraw_hbm, sraw), (states_hbm, states), (wo_hbm, wo),
        (down_hbm, down), (wout_hbm, wout),
    ]
    loads = [pltpu.make_async_copy(src, dst, in_sem.at[n]) for n, (src, dst) in enumerate(pairs)]
    wqk_in, wvz_in, sraw_in, states_in, wo_in, down_in, wout_in = loads

    def raw_in(n):
        return pltpu.make_async_copy(
            win_hbm.at[pl.ds(n * 8192, 8192)], raw.at[n % 2], raw_sem.at[n % 2]
        )

    first = [
        (hid_hbm, hid_ref), (ids_hbm, ids_ref), (wt_hbm, wt_ref), (gain_in_hbm, gain_in), (alog_hbm, alog_ref),
        (dt_hbm, dt_ref), (gain_gate_hbm, gain_gate), (gain_post_hbm, gain_post), (wba_hbm, wba_ref),
        (sgate_hbm, sgate_ref),
    ]
    first = [pltpu.make_async_copy(src, dst, small_sem.at[n]) for n, (src, dst) in enumerate(first)]
    barrier = pltpu.get_barrier_semaphore()
    for i in range(1, HEADS):
        pl.semaphore_signal(barrier, inc=1, device_id=(b, (h + i) % HEADS), device_id_type=MESH)
    for copy in first:
        copy.start()

    @pl.loop(1, BATCH)
    def _(i):
        for to in range(HEADS):
            pl.semaphore_signal(barrier, inc=1, device_id=((b + i) % BATCH, to), device_id_type=MESH)

    for copy in loads[:4]:
        copy.start()
    raw_in(0).start()
    raw_in(1).start()
    for copy in loads[4:]:
        copy.start()

    for copy in first:
        copy.wait()
    pl.semaphore_wait(barrier, DEVS - 1)

    sent = []

    def pass_on(src, slot, to):
        copy = remote(src, hall.at[slot], ag_s.at[len(sent)], ag_r.at[slot], (b, to))
        copy.start()
        sent.append(copy)

    def norm_block(slot):
        rows = rms_scale(hall[slot].astype(F32).reshape(24, 2048), gain_in[...])
        nrm[pl.ds(pl.multiple_of(slot * 24, 8), 24)] = rows

    for d in (2, 1, 3):
        pass_on(hid_ref, h, ((x + d) % 4) * 2 + c)
    pass_on(hid_ref, h, sib)
    to_heads(lambda to: ids_ref, ids_all, i_s, i_r)
    to_heads(lambda to: wt_ref, wts_all, w_s, w_r)
    ids_all[h] = ids_ref[...]
    wts_all[h] = wt_ref[...]
    hall[h] = hid_ref[...]
    norm_block(h)
    wqk_in.wait()
    part_rows(wqk, wide, 2, lambda s: 128 * s, 8)

    def forward(d):
        slot = ((x + d) % 4) * 2 + c
        wait_bytes(hall.at[slot], ag_r.at[slot])
        pass_on(hall.at[slot], slot, sib)

    forward(3)
    forward(1)
    forward(2)
    wvz_in.wait()
    part_rows(wvz, wide, 4, lambda s: 256 + 128 * s, 16)
    for d in (3, 1, 2):
        norm_block(((x + d) % 4) * 2 + c)
    for d in (0, 3, 1, 2):
        slot = ((x + d) % 4) * 2 + 1 - c
        wait_bytes(hall.at[slot], ag_r.at[slot])
        norm_block(slot)

    left = nrm[...].astype(BF16)
    for n in range(3):
        proj[:, 256 * n : 256 * n + 256] = mm(left, wide[:, 256 * n : 256 * n + 256])
    wba = wba_ref[...].astype(F32)
    wba = jnp.concatenate([wba[0], wba[1], jnp.zeros((4, 2048), F32)], axis=0).astype(BF16)
    bas[...] = lax.dot_general(left, wba, (((1,), (1,)), ((), ())), preferred_element_type=F32)

    states_in.wait()
    wo_in.wait()

    def partial_rows(o):
        at = pl.multiple_of(o * 24, 8)
        gated = delta_rows(
            proj[pl.ds(at, 24)], bas[pl.ds(at, 24)], (alog_ref[...], dt_ref[...]), gain_gate[...],
            states[pl.ds(pl.multiple_of(o * 8, 8), 8)],
        )
        gated = jnp.concatenate([gated, jnp.zeros((8, 256), F32)], axis=0).astype(BF16)
        return mm(gated, wo[...])[:24].reshape(3, 8, 2048)

    @pl.loop(0, 3)
    def _(k):
        o = ((x + 1 + k) % 4) * 2 + 1 - c
        partb[o] = partial_rows(o).astype(BF16)
        remote(partb.at[o], fs.at[k], f_s, f_r.at[k], (b, sib)).start()

    @pl.loop(0, 3)
    def _(k):
        o = ((x + 1 + k) % 4) * 2 + c
        rows = partial_rows(o)
        wait_bytes(fs.at[k], f_r.at[k])
        partb[o] = (rows + fs[k].astype(F32)).astype(BF16)
        remote(partb.at[o], rs.at[k], rs_s, rs_r, (b, o)).start()

    partb[sib] = partial_rows(sib).astype(BF16)
    remote(partb.at[sib], rs.at[3], rs_s, rs_r, (b, sib)).start()
    total = partial_rows(h)

    i0, i1 = iota((128, 128), 0), iota((128, 128), 1)
    later = one_hot((i0 // 32 == i1 // 32) & (i1 < i0)).astype(BF16)
    own = jnp.concatenate([ids_ref[...].reshape(24, 10), jnp.full((8, 10), -1, jnp.int32)], axis=0)
    own = jnp.concatenate([own] * 4, axis=0)
    col = iota((128, 256), 1)
    col_chunk, col_rank = (col // 4) % 4, (col % 2).astype(F32)
    named = head_at((col // 16) % 8, 1) * 2 + (col // 2) % 2
    row_chunk = iota((128, 256), 0) // 32

    @pl.loop(0, 8)
    def _(g):
        first, second = batch_at(2 * g, 1) * 16, batch_at(2 * g + 1, 1) * 16
        hot = count_hits(own, named + jnp.where(col < 128, first, second))
        before = mm(later, hot.astype(BF16))
        chosen = jnp.where((before == col_rank) & (row_chunk == col_chunk), hot, 0.0)
        placing[g] = chosen.T.astype(BF16)

    sraw_in.wait()
    part_rows(sraw, swin, 8, gate_up_lane, 4)

    wait_bytes(rs, rs_r)
    for i in range(4):
        total = total + rs[i].astype(F32)
    resid = (hid_ref[...].astype(F32) + total).astype(BF16)
    post = rms_scale(resid.astype(F32), gain_post[...].reshape(1, 1, 2048)).astype(BF16)
    rows = post.astype(F32).reshape(24, 2048)
    blank = jnp.zeros((8, 512), F32)
    stacked[...] = jnp.concatenate(
        [v for j in range(4) for v in (rows[:, 512 * j : 512 * j + 512], blank)], axis=0
    ).astype(BF16)
    for i in range(HEADS):
        psend[i, 0] = resid[:, :, 256 * i : 256 * i + 256]
        psend[i, 1] = post[:, :, 256 * i : 256 * i + 256]
    to_heads(lambda to: psend.at[to], slices, p_s, p_r)
    slices[h] = psend[h]

    for part in range(PARTS):
        @pl.loop(CUTS[part] // 16, CUTS[part + 1] // 16)
        def _(g):
            rows = mm(placing[g], stacked[...]).astype(BF16)
            send[pl.ds(g * 16, 16)] = rows.reshape(16, 16, 512)

        for n in far_first(part):
            if n:
                to = (batch_at(n // 8, 1), head_at(n % 8, 1))
                remote(send.at[n], recv.at[n], d_s, d_r.at[part], to).start()
            else:
                pltpu.make_async_copy(send.at[n], recv.at[n], d_r.at[part]).start()

    def lay_out(n):
        raw_in(n).wait()
        part_rows(raw.at[n % 2], win, 8, gate_up_lane, 16, 0, n * 1024)
        if n < 2:
            raw_in(n + 2).start()

    lay_out(0)
    lay_out(1)
    take(slices, p_r)
    every = slices[:, 1].astype(F32).reshape(192, 256)
    up = mm(every.astype(BF16), swin[...])
    sgate = sgate_ref[...].astype(F32)
    logit = jnp.sum(every[:, :128] * sgate[:1] + every[:, 128:] * sgate[1:], axis=-1, keepdims=True)
    high = logit.astype(BF16).astype(F32)
    zero = jnp.zeros((192, 126), F32)
    sp[...] = (
        jnp.concatenate([up, high, logit - high, zero], axis=1).astype(BF16).reshape(HEADS, 3, 8, 1152)
    )
    to_heads(lambda to: sp.at[to], sp_recv, g_s, g_r)

    lay_out(2)
    lay_out(3)

    take(ids_all, i_r)
    take(wts_all, w_r)
    ids = ids_all[...].reshape(192, 10)
    wts = wts_all[...].reshape(192, 10)
    i0, i1 = iota((192, 192), 0), iota((192, 192), 1)
    later2 = one_hot((i0 // 24 == i1 // 24) & (i1 < i0)).astype(BF16)
    cell = iota((192, 64), 1)
    named2 = head_at((cell // 4) % 8, 1) * 2 + (cell // 2) % 2
    rank2 = (iota((192, 64), 1) % 2).astype(F32)
    widen = one_hot(iota((64, 512), 1) // 8 == iota((64, 512), 0)).astype(BF16)
    col2 = iota((384, 512), 1)
    source_head, member = head_at((col2 // 32) % 8, 1), col2 % 8
    owner = ((source_head // 2 + 4 - member // 2) % 4) * 2 + (source_head + member) % 2
    kept = (iota((384, 512), 0) % 192) // 24 == owner

    @pl.loop(0, 8)
    def _(g):
        near, far = batch_at(2 * g, 1) * 16, batch_at(2 * g + 1, 1) * 16
        here = named2 + jnp.where(cell < 32, near, far)
        hot = jnp.zeros((192, 64), F32)
        heavy = jnp.zeros((192, 64), F32)
        for k in range(10):
            same = ids[:, k : k + 1] == here
            hot = hot + one_hot(same)
            heavy = heavy + jnp.where(same, wts[:, k : k + 1], 0.0)
        before = mm(later2, hot.astype(BF16))
        heavy = jnp.where(before == rank2, heavy, 0.0)
        top = heavy.astype(BF16)
        both = jnp.concatenate([top, (heavy - top.astype(F32)).astype(BF16)], axis=0)
        load[g] = jnp.where(kept, mm(both, widen), 0.0).astype(BF16)

    source, inside = iota((256, 256), 1) // 16, iota((256, 256), 1) % 16
    target = (inside // 4) * 64 + ((inside // 2) % 2) * 32 + (source // 8) * 16 + (inside % 2) * 8 + source % 8
    order = one_hot(iota((256, 256), 0) == target).astype(BF16)
    wout_in.wait()
    for part in range(PARTS):
        start, size = CUTS[part], CUTS[part + 1] - CUTS[part]
        wait_bytes(recv.at[pl.ds(start, size)], d_r.at[part])

        @pl.loop(0, size // 16)
        def _(i):
            got = mm(order, recv[pl.ds(start + i * 16, 16)].reshape(256, 512)).astype(BF16)
            to = pl.multiple_of(i * 32, 32)
            for j in range(4):
                for e in range(2):
                    at = j * 64 + e * 32
                    xs[e, pl.ds(to, 32), 512 * j : 512 * j + 512] = got[at : at + 32]

        @pl.loop(0, 2)
        def _(e):
            inner = []
            for n in range(2):
                lane = slice(256 * n, 256 * n + 256)
                lane2 = slice(512 + 256 * n, 768 + 256 * n)
                gate = mm(xs[e, : 2 * size], win[pl.ds(e * 2048, 2048), lane])
                more = mm(xs[e, : 2 * size], win[pl.ds(e * 2048, 2048), lane2])
                inner.append((silu(gate) * more).astype(BF16))
            inner = jnp.concatenate(inner, axis=1)
            rows = pl.ds(pl.multiple_of(e * 16, 16), 16)
            for f in range(HEADS):
                got = mm(inner, wout[e, :, 256 * f : 256 * f + 256]).astype(BF16)
                for i in range(size // 8):
                    back[start + 8 * i + f, rows, :] = got[16 * i : 16 * i + 16]

        for n in far_first(part):
            batch, f = batch_at(n // 8, -1), head_at(n % 8, -1)
            if n:
                remote(back.at[n // 8 * 8 + f], home.at[n], b_s, b_r.at[part], (batch, f)).start()
            else:
                pltpu.make_async_copy(back.at[f], home.at[n], b_r.at[part]).start()

        if part == 0:
            take(sp_recv, g_r)
            total = sp[h].astype(F32)
            for i in range(1, HEADS):
                total = total + sp_recv[(h + i) % HEADS].astype(F32)
            logit = total[:, :, 1024:1025] + total[:, :, 1025:1026]
            mid = silu(total[:, :, :512]) * total[:, :, 512:1024] * jax.nn.sigmoid(logit)
            mids[h] = mid.astype(BF16)
            to_heads(lambda to: mids.at[h], mids, m_s, m_r)

    down_in.wait()
    take(mids, m_r)
    every = mids[...].astype(F32).reshape(192, 512).astype(BF16)
    shared = mm(every, down[...])
    near = slices[:, 0].astype(F32).reshape(192, 256) + shared
    acc = jnp.zeros((384, 256), F32)
    for part in range(PARTS):
        start, size = CUTS[part], CUTS[part + 1] - CUTS[part]
        wait_bytes(home.at[pl.ds(start, size)], b_r.at[part])
        for g in range(start // 16, (start + size) // 16):
            acc = acc + mm(load[g], home[16 * g : 16 * g + 16].reshape(512, 256))
    acc = acc[:192] + acc[192:]
    out = (near + acc.astype(BF16).astype(F32)).astype(BF16).reshape(HEADS, 3, 8, 256)
    for o in range(HEADS):
        out_ref[:, o] = out[o]
    for copy in sent:
        copy.wait_send()
    take(ids_all, i_s)
    take(wts_all, w_s)
    wait_bytes(fs, f_s)
    wait_bytes(rs, rs_s)
    take(psend, p_s)
    take(send, d_s)
    take(sp, g_s)
    take(mids, m_s)
    take(back, b_s)


def layer(*args):
    dma = pltpu.SemaphoreType.DMA
    return pl.pallas_call(
        layer_kernel,
        name="layer",
        out_shape=jax.ShapeDtypeStruct((3, HEADS, 8, 256), BF16),
        in_specs=[ANY] * 18,
        out_specs=VMEM,
        scratch_shapes=[
            pltpu.VMEM((3, 8, 2048), BF16),
            pltpu.VMEM((3, 8, 10), jnp.int32),
            pltpu.VMEM((3, 8, 10), F32),
            pltpu.VMEM((1, 2048), F32),
            pltpu.VMEM((1, 2), F32),
            pltpu.VMEM((1, 2), F32),
            pltpu.VMEM((1, 128), F32),
            pltpu.VMEM((1, 2048), F32),
            pltpu.VMEM((2, 2, 2048), BF16),
            pltpu.VMEM((2, 128), BF16),
            pltpu.VMEM((HEADS, 3, 8, 2048), BF16),
            pltpu.VMEM((192, 2048), F32),
            pltpu.VMEM((192, 768), F32),
            pltpu.VMEM((192, 8), F32),
            pltpu.VMEM((64, 2, 128, 128), F32),
            pltpu.VMEM((4096, 128), BF16),
            pltpu.VMEM((8192, 128), BF16),
            pltpu.VMEM((2048, 768), BF16),
            pltpu.VMEM((256, 2048), BF16),
            pltpu.VMEM((2048, 128), BF16),
            pltpu.VMEM((256, 1024), BF16),
            pltpu.VMEM((512, 256), BF16),
            pltpu.VMEM((2, 8192, 128), BF16),
            pltpu.VMEM((4096, 1024), BF16),
            pltpu.VMEM((2, 512, 2048), BF16),
            pltpu.VMEM((HEADS, 3, 8, 10), jnp.int32),
            pltpu.VMEM((HEADS, 3, 8, 10), F32),
            pltpu.VMEM((HEADS, 3, 8, 2048), BF16),
            pltpu.VMEM((3, 3, 8, 2048), BF16),
            pltpu.VMEM((4, 3, 8, 2048), BF16),
            pltpu.VMEM((DEVS, 16, 512), BF16),
            pltpu.VMEM((DEVS, 16, 512), BF16),
            pltpu.VMEM((HEADS, 2, 3, 8, 256), BF16),
            pltpu.VMEM((HEADS, 2, 3, 8, 256), BF16),
            pltpu.VMEM((128, 512), BF16),
            pltpu.VMEM((8, 256, 128), BF16),
            pltpu.VMEM((8, 384, 512), BF16),
            pltpu.VMEM((2, 2 * max(b - a for a, b in zip(CUTS, CUTS[1:])), 2048), BF16),
            pltpu.VMEM((DEVS, 32, 256), BF16),
            pltpu.VMEM((DEVS, 32, 256), BF16),
            pltpu.VMEM((HEADS, 3, 8, 1152), BF16),
            pltpu.VMEM((HEADS, 3, 8, 1152), BF16),
            pltpu.VMEM((HEADS, 3, 8, 512), BF16),
            dma((10,)), dma((7,)), dma((2,)), dma((7,)), dma((HEADS,)),
        ]
        + [dma(())] * 5
        + [dma((3,))]
        + [dma(())] * 5
        + [dma((PARTS,)), dma(()), dma((PARTS,))]
        + [dma(())] * 4,
        compiler_params=pltpu.CompilerParams(
            collective_id=0, has_side_effects=True, vmem_limit_bytes=60 * 2**20
        ),
    )(*args)


def column_rows(w):
    return w.reshape(-1, 2, 4, 128).transpose(0, 2, 1, 3).reshape(-1, 128)


def shards(
    hidden_in, states, norm_in, w_qk, w_vz, w_ba, a_log, dt_bias, norm_gate, w_out, norm_post,
    shared_in, shared_gate, shared_out, expert_in, expert_out, routes, route_weight,
):
    out = layer(
        hidden_in.transpose(1, 0, 2),
        routes.transpose(1, 0, 2),
        route_weight.transpose(1, 0, 2),
        norm_in.reshape(1, 2048),
        a_log.reshape(1, 2),
        dt_bias.reshape(1, 2),
        norm_gate.reshape(1, 128),
        norm_post.reshape(1, 2048),
        w_ba.transpose(1, 2, 0),
        shared_gate.reshape(2, 128),
        states,
        w_qk.reshape(4096, 128),
        w_vz.reshape(8192, 128),
        w_out.reshape(256, 2048),
        column_rows(shared_in),
        shared_out,
        column_rows(expert_in),
        expert_out,
    )
    return out.reshape(3, 64, 256).transpose(1, 0, 2)


def solution(mesh):
    in_specs = (
        P(("batch", "head"), None, None),
        P("batch", "head", None, None),
        P(),
        P(None, "head", None, None),
        P(None, "head", None, None),
        P(None, None, "head"),
        P("head"),
        P("head"),
        P(),
        P("head", None, None),
        P(),
        P("head", None, None),
        P("head"),
        P(None, "head"),
        P(("batch", "head"), None, None, None),
        P(("batch", "head"), None, None),
        P(("batch", "head"), None, None),
        P(("batch", "head"), None, None),
    )
    out_specs = P("batch", None, "head")
    return jax.shard_map(shards, mesh=mesh, in_specs=in_specs, out_specs=out_specs, check_vma=False)
```

```python
import jax
import jax.numpy as jnp
from jax import lax
from jax.experimental import pallas as pl
from jax.experimental.pallas import tpu as pltpu
from jax.sharding import PartitionSpec as P

EPS = 1e-06
MESH = pl.DeviceIdType.MESH
HEADS = 8
BATCH = 16
DEVS = HEADS * BATCH
CUTS = (0, 64, 128)
PARTS = len(CUTS) - 1
F32 = jnp.float32
BF16 = jnp.bfloat16
VMEM = pl.BlockSpec(memory_space=pltpu.VMEM)
ANY = pl.BlockSpec(memory_space=pl.ANY)


def rms_scale(values, gain):
    return values * lax.rsqrt(jnp.mean(values * values, axis=-1, keepdims=True) + EPS) * gain


def unit_norm(v):
    return v * lax.rsqrt(jnp.sum(v * v, axis=-1, keepdims=True) + EPS)


def silu(v):
    return v * jax.nn.sigmoid(v)


def iota(shape, axis):
    return lax.broadcasted_iota(jnp.int32, shape, axis)


def mm(left, right):
    return jnp.dot(left, right, preferred_element_type=F32)


def one_hot(mask):
    return jnp.where(mask, 1.0, 0.0)


def spot(p):
    return (p // HEADS, p % HEADS)


def remote(src, dst, send_sem, recv_sem, to):
    return pltpu.make_async_remote_copy(
        src_ref=src, dst_ref=dst, send_sem=send_sem, recv_sem=recv_sem, device_id=to, device_id_type=MESH
    )


def wait_bytes(ref, sem):
    pltpu.make_async_copy(ref, ref, sem).wait()


def take(ref, sem):
    wait_bytes(ref.at[pl.ds(0, ref.shape[0] - 1)], sem)


def plane_offset(place):
    dy = (place % 8) // 2
    return dy, (place % 2) * 2 + (dy + place // 8) % 2


def far_first(part):
    def hops(position):
        dy, dz = plane_offset(position // 8)
        return sum(min(d, 4 - d) for d in (dy, dz, (position % 8) // 2))

    return sorted(range(CUTS[part], CUTS[part + 1]), key=lambda position: (-hops(position), position % 5, position))


def part_rows(raw, wide, kinds, lane_of, blocks, from_row=0, to_row=0):
    count = 256 // kinds
    order = one_hot(iota((256, 256), 1) == (iota((256, 256), 0) % count) * kinds + iota((256, 256), 0) // count)
    order = order.astype(BF16)

    @pl.loop(0, blocks, unroll=4)
    def _(i):
        at = pl.multiple_of(from_row + i * 512, 512)
        to = pl.multiple_of(to_row + i * 2 * count, 2 * count)
        pair = jnp.concatenate([raw[pl.ds(at, 256)], raw[pl.ds(at + 256, 256)]], axis=1)
        got = mm(order, pair).astype(BF16)
        for s in range(kinds):
            lane = lane_of(s)
            part = got[count * s : count * s + count]
            wide[pl.ds(to, count), lane : lane + 128] = part[:, :128]
            wide[pl.ds(to + count, count), lane : lane + 128] = part[:, 128:]


def gate_up_lane(s):
    return (s % 2) * 512 + (s // 2) * 128


def count_hits(ids, here):
    hot = jnp.zeros(here.shape, F32)
    for k in range(10):
        hot = hot + one_hot(ids[:, k : k + 1] == here)
    return hot


def delta_rows(rows, ba, rates, gain, states):
    q = unit_norm(silu(rows[:, :128])) * (128 ** -0.5)
    k = unit_norm(silu(rows[:, 128:256]))
    left = jnp.concatenate([k, q], axis=0)
    place = iota((48, 128), 0) % 8
    left = jnp.concatenate([jnp.where(place == s, left, 0.0) for s in range(8)], axis=1)
    right = jnp.concatenate(
        [states[:, 0].reshape(1024, 128), states[:, 1].reshape(1024, 128)], axis=1
    ).astype(BF16)
    met = mm(left.astype(BF16), right)
    q = [q[8 * t : 8 * t + 8] for t in range(3)]
    k = [k[8 * t : 8 * t + 8] for t in range(3)]

    def along(u, v):
        return jnp.sum(u * v, axis=-1, keepdims=True)

    kk = {(i, t): along(k[i], k[t]) for i in range(3) for t in range(i + 1, 3)}
    kq = {(i, t): along(k[i], q[t]) for i in range(3) for t in range(i, 3)}
    heads = []
    for j in range(2):
        lane = slice(128 * j, 128 * j + 128)
        values = silu(rows[:, 256 + 256 * j : 384 + 256 * j])
        gate_z = silu(rows[:, 384 + 256 * j : 512 + 256 * j])
        raw = ba[:, 2 + j : 3 + j] + rates[1][:, j : j + 1]
        decays = jnp.exp(-jnp.exp(rates[0][:, j : j + 1]) * jax.nn.softplus(raw))
        betas = jax.nn.sigmoid(ba[:, j : j + 1])
        decay = [decays[8 * t : 8 * t + 8] for t in range(3)]
        deltas, steps = [], []
        for t in range(3):
            whole = decay[0]
            for i in range(1, t + 1):
                whole = whole * decay[i]
            recalled = whole * met[8 * t : 8 * t + 8, lane]
            readout = whole * met[24 + 8 * t : 32 + 8 * t, lane]
            fade = jnp.ones_like(whole)
            for i in range(t - 1, -1, -1):
                fade = fade * decay[i + 1]
                recalled = recalled + (fade * kk[i, t]) * deltas[i]
                readout = readout + (fade * kq[i, t]) * deltas[i]
            deltas.append(betas[8 * t : 8 * t + 8] * (values[8 * t : 8 * t + 8] - recalled))
            readout = readout + kq[t, t] * deltas[t]
            steps.append(rms_scale(readout, gain) * gate_z[8 * t : 8 * t + 8])
        heads.append(jnp.concatenate(steps, axis=0))
    return jnp.concatenate(heads, axis=1)


def layer_kernel(
    hid_hbm, ids_hbm, wt_hbm, gain_in_hbm, alog_hbm, dt_hbm, gain_gate_hbm, gain_post_hbm, wba_hbm, sgate_hbm,
    states_hbm, wqk_hbm, wvz_hbm, wo_hbm, sraw_hbm, down_hbm, win_hbm, wout_hbm,
    out_ref,
    hid_ref, ids_ref, wt_ref, gain_in, alog_ref, dt_ref, gain_gate, gain_post, wba_ref, sgate_ref, hall, nrm, proj, bas, states, wqk, wvz, wide, wo, sraw, swin, down, raw, win, wout,
    ids_all, wts_all, partb, fs, rs, send, recv, psend, slices, stacked, placing, load, xs,
    back, home, sp, sp_recv, mids,
    small_sem, in_sem, raw_sem, ag_s, ag_r, i_s, i_r, w_s, w_r, f_s, f_r, rs_s, rs_r, p_s, p_r, d_s, d_r, b_s, b_r, g_s, g_r, m_s, m_r,
):
    b = lax.axis_index("batch")
    h = lax.axis_index("head")
    p = b * HEADS + h
    x, c = h // 2, h % 2
    sib = x * 2 + 1 - c
    y, z = b // 4, b % 4

    def batch_at(place, sign):
        dy, dz = plane_offset(place)
        return ((y + 4 + sign * dy) % 4) * 4 + (z + 4 + sign * dz) % 4

    def head_at(member, sign):
        return ((x + 4 + sign * (member // 2)) % 4) * 2 + (c + member) % 2

    def to_heads(src, dst, ssem, rsem):
        for i in range(1, HEADS):
            to = (h + i) % HEADS
            remote(src(to), dst.at[h], ssem, rsem, (b, to)).start()

    pairs = [
        (wqk_hbm, wqk), (wvz_hbm, wvz), (sraw_hbm, sraw), (states_hbm, states), (wo_hbm, wo),
        (down_hbm, down), (wout_hbm, wout),
    ]
    loads = [pltpu.make_async_copy(src, dst, in_sem.at[n]) for n, (src, dst) in enumerate(pairs)]
    wqk_in, wvz_in, sraw_in, states_in, wo_in, down_in, wout_in = loads

    def raw_in(n):
        return pltpu.make_async_copy(
            win_hbm.at[pl.ds(n * 8192, 8192)], raw.at[n % 2], raw_sem.at[n % 2]
        )

    first = [
        (hid_hbm, hid_ref), (ids_hbm, ids_ref), (wt_hbm, wt_ref), (gain_in_hbm, gain_in), (alog_hbm, alog_ref),
        (dt_hbm, dt_ref), (gain_gate_hbm, gain_gate), (gain_post_hbm, gain_post), (wba_hbm, wba_ref),
        (sgate_hbm, sgate_ref),
    ]
    first = [pltpu.make_async_copy(src, dst, small_sem.at[n]) for n, (src, dst) in enumerate(first)]
    barrier = pltpu.get_barrier_semaphore()
    for i in range(1, HEADS):
        pl.semaphore_signal(barrier, inc=1, device_id=(b, (h + i) % HEADS), device_id_type=MESH)
    for copy in first:
        copy.start()

    @pl.loop(1, BATCH)
    def _(i):
        for to in range(HEADS):
            pl.semaphore_signal(barrier, inc=1, device_id=((b + i) % BATCH, to), device_id_type=MESH)

    for copy in loads[:4]:
        copy.start()
    raw_in(0).start()
    raw_in(1).start()
    for copy in loads[4:]:
        copy.start()

    for copy in first:
        copy.wait()
    pl.semaphore_wait(barrier, DEVS - 1)

    sent = []

    def pass_on(src, slot, to):
        copy = remote(src, hall.at[slot], ag_s.at[len(sent)], ag_r.at[slot], (b, to))
        copy.start()
        sent.append(copy)

    def norm_block(slot):
        rows = rms_scale(hall[slot].astype(F32).reshape(24, 2048), gain_in[...])
        nrm[pl.ds(pl.multiple_of(slot * 24, 8), 24)] = rows

    for d in (2, 1, 3):
        pass_on(hid_ref, h, ((x + d) % 4) * 2 + c)
    pass_on(hid_ref, h, sib)
    to_heads(lambda to: ids_ref, ids_all, i_s, i_r)
    to_heads(lambda to: wt_ref, wts_all, w_s, w_r)
    ids_all[h] = ids_ref[...]
    wts_all[h] = wt_ref[...]
    hall[h] = hid_ref[...]
    norm_block(h)
    wqk_in.wait()
    part_rows(wqk, wide, 2, lambda s: 128 * s, 8)

    def forward(d):
        slot = ((x + d) % 4) * 2 + c
        wait_bytes(hall.at[slot], ag_r.at[slot])
        pass_on(hall.at[slot], slot, sib)

    forward(3)
    forward(1)
    forward(2)
    wvz_in.wait()
    part_rows(wvz, wide, 4, lambda s: 256 + 128 * s, 16)
    for d in (3, 1, 2):
        norm_block(((x + d) % 4) * 2 + c)
    for d in (0, 3, 1, 2):
        slot = ((x + d) % 4) * 2 + 1 - c
        wait_bytes(hall.at[slot], ag_r.at[slot])
        norm_block(slot)

    left = nrm[...].astype(BF16)
    for n in range(3):
        proj[:, 256 * n : 256 * n + 256] = mm(left, wide[:, 256 * n : 256 * n + 256])
    wba = wba_ref[...].astype(F32)
    wba = jnp.concatenate([wba[0], wba[1], jnp.zeros((4, 2048), F32)], axis=0).astype(BF16)
    bas[...] = lax.dot_general(left, wba, (((1,), (1,)), ((), ())), preferred_element_type=F32)

    states_in.wait()
    wo_in.wait()

    def gated_rows(o):
        at = pl.multiple_of(o * 24, 8)
        return delta_rows(
            proj[pl.ds(at, 24)], bas[pl.ds(at, 24)], (alog_ref[...], dt_ref[...]), gain_gate[...],
            states[pl.ds(pl.multiple_of(o * 8, 8), 8)],
        )

    def partial_rows(o):
        gated = jnp.concatenate([gated_rows(o), jnp.zeros((8, 256), F32)], axis=0).astype(BF16)
        return mm(gated, wo[...])[:24].reshape(3, 8, 2048)

    others = [((x + d) % 4) * 2 + 1 - c for d in (2, 1, 3)]
    gated = jnp.concatenate([gated_rows(o) for o in others] + [jnp.zeros((24, 256), F32)], axis=0)
    rows = mm(gated.astype(BF16), wo[...])
    for k, o in enumerate(others):
        partb[o] = rows[24 * k : 24 * k + 24].reshape(3, 8, 2048).astype(BF16)
        remote(partb.at[o], fs.at[k], f_s, f_r.at[k], (b, sib)).start()

    @pl.loop(0, 3)
    def _(k):
        o = ((x + 2 - k + 3 * (k // 2)) % 4) * 2 + c
        rows = partial_rows(o)
        wait_bytes(fs.at[k], f_r.at[k])
        partb[o] = (rows + fs[k].astype(F32)).astype(BF16)
        remote(partb.at[o], rs.at[k], rs_s, rs_r, (b, o)).start()

    partb[sib] = partial_rows(sib).astype(BF16)
    remote(partb.at[sib], rs.at[3], rs_s, rs_r, (b, sib)).start()
    total = partial_rows(h)

    i0, i1 = iota((128, 128), 0), iota((128, 128), 1)
    later = one_hot((i0 // 32 == i1 // 32) & (i1 < i0)).astype(BF16)
    own = jnp.concatenate([ids_ref[...].reshape(24, 10), jnp.full((8, 10), -1, jnp.int32)], axis=0)
    own = jnp.concatenate([own] * 4, axis=0)
    col = iota((128, 256), 1)
    col_chunk, col_rank = (col // 4) % 4, (col % 2).astype(F32)
    named = head_at((col // 16) % 8, 1) * 2 + (col // 2) % 2
    row_chunk = iota((128, 256), 0) // 32

    @pl.loop(0, 8)
    def _(g):
        first, second = batch_at(2 * g, 1) * 16, batch_at(2 * g + 1, 1) * 16
        hot = count_hits(own, named + jnp.where(col < 128, first, second))
        before = mm(later, hot.astype(BF16))
        chosen = jnp.where((before == col_rank) & (row_chunk == col_chunk), hot, 0.0)
        placing[g] = chosen.T.astype(BF16)

    sraw_in.wait()
    part_rows(sraw, swin, 8, gate_up_lane, 4)

    wait_bytes(rs, rs_r)
    for i in range(4):
        total = total + rs[i].astype(F32)
    resid = (hid_ref[...].astype(F32) + total).astype(BF16)
    post = rms_scale(resid.astype(F32), gain_post[...].reshape(1, 1, 2048)).astype(BF16)
    rows = post.astype(F32).reshape(24, 2048)
    blank = jnp.zeros((8, 512), F32)
    stacked[...] = jnp.concatenate(
        [v for j in range(4) for v in (rows[:, 512 * j : 512 * j + 512], blank)], axis=0
    ).astype(BF16)

    for i in range(HEADS):
        psend[i, 0] = resid[:, :, 256 * i : 256 * i + 256]
        psend[i, 1] = post[:, :, 256 * i : 256 * i + 256]
    to_heads(lambda to: psend.at[to], slices, p_s, p_r)
    slices[h] = psend[h]

    for part in range(PARTS):
        @pl.loop(CUTS[part] // 16, CUTS[part + 1] // 16)
        def _(g):
            rows = mm(placing[g], stacked[...]).astype(BF16)
            send[pl.ds(g * 16, 16)] = rows.reshape(16, 16, 512)

        for n in far_first(part):
            if n:
                to = (batch_at(n // 8, 1), head_at(n % 8, 1))
                remote(send.at[n], recv.at[n], d_s, d_r.at[part], to).start()
            else:
                pltpu.make_async_copy(send.at[n], recv.at[n], d_r.at[part]).start()


    def lay_out(n):
        raw_in(n).wait()
        part_rows(raw.at[n % 2], win, 8, gate_up_lane, 16, 0, n * 1024)
        if n < 2:
            raw_in(n + 2).start()

    lay_out(0)
    lay_out(1)
    take(slices, p_r)
    every = slices[:, 1].astype(F32).reshape(192, 256)
    up = mm(every.astype(BF16), swin[...])
    sgate = sgate_ref[...].astype(F32)
    logit = jnp.sum(every[:, :128] * sgate[:1] + every[:, 128:] * sgate[1:], axis=-1, keepdims=True)
    high = logit.astype(BF16).astype(F32)
    zero = jnp.zeros((192, 126), F32)
    sp[...] = (
        jnp.concatenate([up, high, logit - high, zero], axis=1).astype(BF16).reshape(HEADS, 3, 8, 1152)
    )
    to_heads(lambda to: sp.at[to], sp_recv, g_s, g_r)

    lay_out(2)
    lay_out(3)

    take(ids_all, i_r)
    take(wts_all, w_r)
    ids = ids_all[...].reshape(192, 10)
    wts = wts_all[...].reshape(192, 10)
    i0, i1 = iota((192, 192), 0), iota((192, 192), 1)
    later2 = one_hot((i0 // 24 == i1 // 24) & (i1 < i0)).astype(BF16)
    cell = iota((192, 64), 1)
    named2 = head_at((cell // 4) % 8, 1) * 2 + (cell // 2) % 2
    rank2 = (iota((192, 64), 1) % 2).astype(F32)
    widen = one_hot(iota((64, 512), 1) // 8 == iota((64, 512), 0)).astype(BF16)
    col2 = iota((384, 512), 1)
    source_head, member = head_at((col2 // 32) % 8, 1), col2 % 8
    owner = ((source_head // 2 + 4 - member // 2) % 4) * 2 + (source_head + member) % 2
    kept = (iota((384, 512), 0) % 192) // 24 == owner

    @pl.loop(0, 8)
    def _(g):
        near, far = batch_at(2 * g, 1) * 16, batch_at(2 * g + 1, 1) * 16
        here = named2 + jnp.where(cell < 32, near, far)
        hot = jnp.zeros((192, 64), F32)
        heavy = jnp.zeros((192, 64), F32)
        for k in range(10):
            same = ids[:, k : k + 1] == here
            hot = hot + one_hot(same)
            heavy = heavy + jnp.where(same, wts[:, k : k + 1], 0.0)
        before = mm(later2, hot.astype(BF16))
        heavy = jnp.where(before == rank2, heavy, 0.0)
        top = heavy.astype(BF16)
        both = jnp.concatenate([top, (heavy - top.astype(F32)).astype(BF16)], axis=0)
        load[g] = jnp.where(kept, mm(both, widen), 0.0).astype(BF16)

    source, inside = iota((256, 256), 1) // 16, iota((256, 256), 1) % 16
    target = (inside // 4) * 64 + ((inside // 2) % 2) * 32 + (source // 8) * 16 + (inside % 2) * 8 + source % 8
    order = one_hot(iota((256, 256), 0) == target).astype(BF16)
    wout_in.wait()
    for part in range(PARTS):
        start, size = CUTS[part], CUTS[part + 1] - CUTS[part]
        wait_bytes(recv.at[pl.ds(start, size)], d_r.at[part])

        @pl.loop(0, size // 16)
        def _(i):
            got = mm(order, recv[pl.ds(start + i * 16, 16)].reshape(256, 512)).astype(BF16)
            to = pl.multiple_of(i * 32, 32)
            for j in range(4):
                for e in range(2):
                    at = j * 64 + e * 32
                    xs[e, pl.ds(to, 32), 512 * j : 512 * j + 512] = got[at : at + 32]

        @pl.loop(0, 2)
        def _(e):
            inner = []
            for n in range(2):
                lane = slice(256 * n, 256 * n + 256)
                lane2 = slice(512 + 256 * n, 768 + 256 * n)
                gate = mm(xs[e, : 2 * size], win[pl.ds(e * 2048, 2048), lane])
                more = mm(xs[e, : 2 * size], win[pl.ds(e * 2048, 2048), lane2])
                inner.append((silu(gate) * more).astype(BF16))
            inner = jnp.concatenate(inner, axis=1)
            rows = pl.ds(pl.multiple_of(e * 16, 16), 16)
            for f in range(HEADS):
                got = mm(inner, wout[e, :, 256 * f : 256 * f + 256]).astype(BF16)
                for i in range(size // 8):
                    back[start + 8 * i + f, rows, :] = got[16 * i : 16 * i + 16]

        for n in far_first(part):
            batch, f = batch_at(n // 8, -1), head_at(n % 8, -1)
            if n:
                remote(back.at[n // 8 * 8 + f], home.at[n], b_s, b_r.at[part], (batch, f)).start()
            else:
                pltpu.make_async_copy(back.at[f], home.at[n], b_r.at[part]).start()

        if part == 0:
            take(sp_recv, g_r)
            total = sp[h].astype(F32)
            for i in range(1, HEADS):
                total = total + sp_recv[(h + i) % HEADS].astype(F32)
            logit = total[:, :, 1024:1025] + total[:, :, 1025:1026]
            mid = silu(total[:, :, :512]) * total[:, :, 512:1024] * jax.nn.sigmoid(logit)
            mids[h] = mid.astype(BF16)
            to_heads(lambda to: mids.at[h], mids, m_s, m_r)

    down_in.wait()
    take(mids, m_r)
    every = mids[...].astype(F32).reshape(192, 512).astype(BF16)
    shared = mm(every, down[...])
    near = slices[:, 0].astype(F32).reshape(192, 256) + shared
    acc = jnp.zeros((384, 256), F32)
    for part in range(PARTS):
        start, size = CUTS[part], CUTS[part + 1] - CUTS[part]
        wait_bytes(home.at[pl.ds(start, size)], b_r.at[part])
        for g in range(start // 16, (start + size) // 16):
            acc = acc + mm(load[g], home[16 * g : 16 * g + 16].reshape(512, 256))
    acc = acc[:192] + acc[192:]
    out = (near + acc.astype(BF16).astype(F32)).astype(BF16).reshape(HEADS, 3, 8, 256)
    for o in range(HEADS):
        out_ref[:, o] = out[o]
    for copy in sent:
        copy.wait_send()
    take(ids_all, i_s)
    take(wts_all, w_s)
    wait_bytes(fs, f_s)
    wait_bytes(rs, rs_s)
    take(psend, p_s)
    take(send, d_s)
    take(sp, g_s)
    take(mids, m_s)
    take(back, b_s)


def layer(*args):
    dma = pltpu.SemaphoreType.DMA
    return pl.pallas_call(
        layer_kernel,
        name="layer",
        out_shape=jax.ShapeDtypeStruct((3, HEADS, 8, 256), BF16),
        in_specs=[ANY] * 18,
        out_specs=VMEM,
        scratch_shapes=[
            pltpu.VMEM((3, 8, 2048), BF16),
            pltpu.VMEM((3, 8, 10), jnp.int32),
            pltpu.VMEM((3, 8, 10), F32),
            pltpu.VMEM((1, 2048), F32),
            pltpu.VMEM((1, 2), F32),
            pltpu.VMEM((1, 2), F32),
            pltpu.VMEM((1, 128), F32),
            pltpu.VMEM((1, 2048), F32),
            pltpu.VMEM((2, 2, 2048), BF16),
            pltpu.VMEM((2, 128), BF16),
            pltpu.VMEM((HEADS, 3, 8, 2048), BF16),
            pltpu.VMEM((192, 2048), F32),
            pltpu.VMEM((192, 768), F32),
            pltpu.VMEM((192, 8), F32),
            pltpu.VMEM((64, 2, 128, 128), F32),
            pltpu.VMEM((4096, 128), BF16),
            pltpu.VMEM((8192, 128), BF16),
            pltpu.VMEM((2048, 768), BF16),
            pltpu.VMEM((256, 2048), BF16),
            pltpu.VMEM((2048, 128), BF16),
            pltpu.VMEM((256, 1024), BF16),
            pltpu.VMEM((512, 256), BF16),
            pltpu.VMEM((2, 8192, 128), BF16),
            pltpu.VMEM((4096, 1024), BF16),
            pltpu.VMEM((2, 512, 2048), BF16),
            pltpu.VMEM((HEADS, 3, 8, 10), jnp.int32),
            pltpu.VMEM((HEADS, 3, 8, 10), F32),
            pltpu.VMEM((HEADS, 3, 8, 2048), BF16),
            pltpu.VMEM((3, 3, 8, 2048), BF16),
            pltpu.VMEM((4, 3, 8, 2048), BF16),
            pltpu.VMEM((DEVS, 16, 512), BF16),
            pltpu.VMEM((DEVS, 16, 512), BF16),
            pltpu.VMEM((HEADS, 2, 3, 8, 256), BF16),
            pltpu.VMEM((HEADS, 2, 3, 8, 256), BF16),
            pltpu.VMEM((128, 512), BF16),
            pltpu.VMEM((8, 256, 128), BF16),
            pltpu.VMEM((8, 384, 512), BF16),
            pltpu.VMEM((2, 2 * max(b - a for a, b in zip(CUTS, CUTS[1:])), 2048), BF16),
            pltpu.VMEM((DEVS, 32, 256), BF16),
            pltpu.VMEM((DEVS, 32, 256), BF16),
            pltpu.VMEM((HEADS, 3, 8, 1152), BF16),
            pltpu.VMEM((HEADS, 3, 8, 1152), BF16),
            pltpu.VMEM((HEADS, 3, 8, 512), BF16),
            dma((10,)), dma((7,)), dma((2,)), dma((7,)), dma((HEADS,)),
        ]
        + [dma(())] * 5
        + [dma((3,))]
        + [dma(())] * 5
        + [dma((PARTS,)), dma(()), dma((PARTS,))]
        + [dma(())] * 4,
        compiler_params=pltpu.CompilerParams(
            collective_id=0, has_side_effects=True, vmem_limit_bytes=60 * 2**20
        ),
    )(*args)


def column_rows(w):
    return w.reshape(-1, 2, 4, 128).transpose(0, 2, 1, 3).reshape(-1, 128)


def shards(
    hidden_in, states, norm_in, w_qk, w_vz, w_ba, a_log, dt_bias, norm_gate, w_out, norm_post,
    shared_in, shared_gate, shared_out, expert_in, expert_out, routes, route_weight,
):
    out = layer(
        hidden_in.transpose(1, 0, 2),
        routes.transpose(1, 0, 2),
        route_weight.transpose(1, 0, 2),
        norm_in.reshape(1, 2048),
        a_log.reshape(1, 2),
        dt_bias.reshape(1, 2),
        norm_gate.reshape(1, 128),
        norm_post.reshape(1, 2048),
        w_ba.transpose(1, 2, 0),
        shared_gate.reshape(2, 128),
        states,
        w_qk.reshape(4096, 128),
        w_vz.reshape(8192, 128),
        w_out.reshape(256, 2048),
        column_rows(shared_in),
        shared_out,
        column_rows(expert_in),
        expert_out,
    )
    return out.reshape(3, 64, 256).transpose(1, 0, 2)


def solution(mesh):
    in_specs = (
        P(("batch", "head"), None, None),
        P("batch", "head", None, None),
        P(),
        P(None, "head", None, None),
        P(None, "head", None, None),
        P(None, None, "head"),
        P("head"),
        P("head"),
        P(),
        P("head", None, None),
        P(),
        P("head", None, None),
        P("head"),
        P(None, "head"),
        P(("batch", "head"), None, None, None),
        P(("batch", "head"), None, None),
        P(("batch", "head"), None, None),
        P(("batch", "head"), None, None),
    )
    out_specs = P("batch", None, "head")
    return jax.shard_map(shards, mesh=mesh, in_specs=in_specs, out_specs=out_specs, check_vma=False)
```

```python
import jax
import jax.numpy as jnp
from jax import lax
from jax.experimental import pallas as pl
from jax.experimental.pallas import tpu as pltpu
from jax.sharding import PartitionSpec as P

EPS = 1e-06
MESH = pl.DeviceIdType.MESH
HEADS = 8
BATCH = 16
DEVS = HEADS * BATCH
CUTS = (0, 64, 128)
PARTS = len(CUTS) - 1
F32 = jnp.float32
BF16 = jnp.bfloat16
VMEM = pl.BlockSpec(memory_space=pltpu.VMEM)
ANY = pl.BlockSpec(memory_space=pl.ANY)


def rms_scale(values, gain):
    return values * lax.rsqrt(jnp.mean(values * values, axis=-1, keepdims=True) + EPS) * gain


def unit_norm(v):
    return v * lax.rsqrt(jnp.sum(v * v, axis=-1, keepdims=True) + EPS)


def silu(v):
    return v * jax.nn.sigmoid(v)


def iota(shape, axis):
    return lax.broadcasted_iota(jnp.int32, shape, axis)


def mm(left, right):
    return jnp.dot(left, right, preferred_element_type=F32)


def one_hot(mask):
    return jnp.where(mask, 1.0, 0.0)


def spot(p):
    return (p // HEADS, p % HEADS)


def remote(src, dst, send_sem, recv_sem, to):
    return pltpu.make_async_remote_copy(
        src_ref=src, dst_ref=dst, send_sem=send_sem, recv_sem=recv_sem, device_id=to, device_id_type=MESH
    )


def wait_bytes(ref, sem):
    pltpu.make_async_copy(ref, ref, sem).wait()


def take(ref, sem):
    wait_bytes(ref.at[pl.ds(0, ref.shape[0] - 1)], sem)


def plane_offset(place):
    dy = (place % 8) // 2
    return dy, (place % 2) * 2 + (dy + place // 8) % 2


def far_first(part):
    def hops(position):
        dy, dz = plane_offset(position // 8)
        return sum(min(d, 4 - d) for d in (dy, dz, (position % 8) // 2))

    return sorted(range(CUTS[part], CUTS[part + 1]), key=lambda position: (-hops(position), position % 5, position))


def part_rows(raw, wide, kinds, lane_of, blocks, from_row=0, to_row=0):
    count = 256 // kinds
    order = one_hot(iota((256, 256), 1) == (iota((256, 256), 0) % count) * kinds + iota((256, 256), 0) // count)
    order = order.astype(BF16)

    @pl.loop(0, blocks, unroll=4)
    def _(i):
        at = pl.multiple_of(from_row + i * 512, 512)
        to = pl.multiple_of(to_row + i * 2 * count, 2 * count)
        pair = jnp.concatenate([raw[pl.ds(at, 256)], raw[pl.ds(at + 256, 256)]], axis=1)
        got = mm(order, pair).astype(BF16)
        for s in range(kinds):
            lane = lane_of(s)
            part = got[count * s : count * s + count]
            wide[pl.ds(to, count), lane : lane + 128] = part[:, :128]
            wide[pl.ds(to + count, count), lane : lane + 128] = part[:, 128:]


def gate_up_lane(s):
    return (s % 2) * 512 + (s // 2) * 128


def count_hits(ids, here):
    hot = jnp.zeros(here.shape, F32)
    for k in range(10):
        hot = hot + one_hot(ids[:, k : k + 1] == here)
    return hot


def delta_rows(rows, ba, rates, gain, states):
    q = unit_norm(silu(rows[:, :128])) * (128 ** -0.5)
    k = unit_norm(silu(rows[:, 128:256]))
    left = jnp.concatenate([k, q], axis=0)
    place = iota((48, 128), 0) % 8
    left = jnp.concatenate([jnp.where(place == s, left, 0.0) for s in range(8)], axis=1)
    right = jnp.concatenate(
        [states[:, 0].reshape(1024, 128), states[:, 1].reshape(1024, 128)], axis=1
    ).astype(BF16)
    met = mm(left.astype(BF16), right)
    q = [q[8 * t : 8 * t + 8] for t in range(3)]
    k = [k[8 * t : 8 * t + 8] for t in range(3)]

    def along(u, v):
        return jnp.sum(u * v, axis=-1, keepdims=True)

    kk = {(i, t): along(k[i], k[t]) for i in range(3) for t in range(i + 1, 3)}
    kq = {(i, t): along(k[i], q[t]) for i in range(3) for t in range(i, 3)}
    heads = []
    for j in range(2):
        lane = slice(128 * j, 128 * j + 128)
        values = silu(rows[:, 256 + 256 * j : 384 + 256 * j])
        gate_z = silu(rows[:, 384 + 256 * j : 512 + 256 * j])
        raw = ba[:, 2 + j : 3 + j] + rates[1][:, j : j + 1]
        decays = jnp.exp(-jnp.exp(rates[0][:, j : j + 1]) * jax.nn.softplus(raw))
        betas = jax.nn.sigmoid(ba[:, j : j + 1])
        decay = [decays[8 * t : 8 * t + 8] for t in range(3)]
        deltas, steps = [], []
        for t in range(3):
            whole = decay[0]
            for i in range(1, t + 1):
                whole = whole * decay[i]
            recalled = whole * met[8 * t : 8 * t + 8, lane]
            readout = whole * met[24 + 8 * t : 32 + 8 * t, lane]
            fade = jnp.ones_like(whole)
            for i in range(t - 1, -1, -1):
                fade = fade * decay[i + 1]
                recalled = recalled + (fade * kk[i, t]) * deltas[i]
                readout = readout + (fade * kq[i, t]) * deltas[i]
            deltas.append(betas[8 * t : 8 * t + 8] * (values[8 * t : 8 * t + 8] - recalled))
            readout = readout + kq[t, t] * deltas[t]
            steps.append(rms_scale(readout, gain) * gate_z[8 * t : 8 * t + 8])
        heads.append(jnp.concatenate(steps, axis=0))
    return jnp.concatenate(heads, axis=1)


def layer_kernel(
    hid_hbm, ids_hbm, wt_hbm, gain_in_hbm, alog_hbm, dt_hbm, gain_gate_hbm, gain_post_hbm, wba_hbm, sgate_hbm,
    states_hbm, wqk_hbm, wvz_hbm, wo_hbm, sraw_hbm, down_hbm, win_hbm, wout_hbm,
    out_ref,
    hid_ref, ids_ref, wt_ref, gain_in, alog_ref, dt_ref, gain_gate, gain_post, wba_ref, sgate_ref, hall, nrm, proj, bas, states, wqk, wvz, wide, wo, sraw, swin, down, raw, win, wout,
    ids_all, wts_all, partb, fs, rs, send, recv, psend, slices, stacked, placing, load, xs, inner,
    back, home, sp, sp_recv, mids,
    small_sem, in_sem, raw_sem, ag_s, ag_r, i_s, i_r, w_s, w_r, f_s, f_r, rs_s, rs_r, p_s, p_r, d_s, d_r, b_s, b_r, g_s, g_r, m_s, m_r,
):
    b = lax.axis_index("batch")
    h = lax.axis_index("head")
    p = b * HEADS + h
    x, c = h // 2, h % 2
    sib = x * 2 + 1 - c
    y, z = b // 4, b % 4

    def batch_at(place, sign):
        dy, dz = plane_offset(place)
        return ((y + 4 + sign * dy) % 4) * 4 + (z + 4 + sign * dz) % 4

    def head_at(member, sign):
        return ((x + 4 + sign * (member // 2)) % 4) * 2 + (c + member) % 2

    def to_heads(src, dst, ssem, rsem):
        for i in range(1, HEADS):
            to = (h + i) % HEADS
            remote(src(to), dst.at[h], ssem, rsem, (b, to)).start()

    pairs = [
        (wqk_hbm, wqk), (wvz_hbm, wvz), (sraw_hbm, sraw), (states_hbm, states), (wo_hbm, wo),
        (down_hbm, down), (wout_hbm, wout),
    ]
    loads = [pltpu.make_async_copy(src, dst, in_sem.at[n]) for n, (src, dst) in enumerate(pairs)]
    wqk_in, wvz_in, sraw_in, states_in, wo_in, down_in, wout_in = loads

    def raw_in(n):
        return pltpu.make_async_copy(
            win_hbm.at[pl.ds(n * 8192, 8192)], raw.at[n % 2], raw_sem.at[n % 2]
        )

    first = [
        (hid_hbm, hid_ref), (ids_hbm, ids_ref), (wt_hbm, wt_ref), (gain_in_hbm, gain_in), (alog_hbm, alog_ref),
        (dt_hbm, dt_ref), (gain_gate_hbm, gain_gate), (gain_post_hbm, gain_post), (wba_hbm, wba_ref),
        (sgate_hbm, sgate_ref),
    ]
    first = [pltpu.make_async_copy(src, dst, small_sem.at[n]) for n, (src, dst) in enumerate(first)]
    barrier = pltpu.get_barrier_semaphore()
    for i in range(1, HEADS):
        pl.semaphore_signal(barrier, inc=1, device_id=(b, (h + i) % HEADS), device_id_type=MESH)
    for copy in first:
        copy.start()

    @pl.loop(1, BATCH)
    def _(i):
        for to in range(HEADS):
            pl.semaphore_signal(barrier, inc=1, device_id=((b + i) % BATCH, to), device_id_type=MESH)

    for copy in loads[:4]:
        copy.start()
    raw_in(0).start()
    raw_in(1).start()
    for copy in loads[4:]:
        copy.start()

    for copy in first:
        copy.wait()
    pl.semaphore_wait(barrier, DEVS - 1)

    sent = []

    def pass_on(src, slot, to):
        copy = remote(src, hall.at[slot], ag_s.at[len(sent)], ag_r.at[slot], (b, to))
        copy.start()
        sent.append(copy)

    def norm_block(slot):
        rows = rms_scale(hall[slot].astype(F32).reshape(24, 2048), gain_in[...])
        nrm[pl.ds(pl.multiple_of(slot * 24, 8), 24)] = rows

    for d in (2, 1, 3):
        pass_on(hid_ref, h, ((x + d) % 4) * 2 + c)
    pass_on(hid_ref, h, sib)
    to_heads(lambda to: ids_ref, ids_all, i_s, i_r)
    to_heads(lambda to: wt_ref, wts_all, w_s, w_r)
    ids_all[h] = ids_ref[...]
    wts_all[h] = wt_ref[...]
    hall[h] = hid_ref[...]
    norm_block(h)
    wqk_in.wait()
    part_rows(wqk, wide, 2, lambda s: 128 * s, 8)

    def forward(d):
        slot = ((x + d) % 4) * 2 + c
        wait_bytes(hall.at[slot], ag_r.at[slot])
        pass_on(hall.at[slot], slot, sib)

    forward(3)
    forward(1)
    forward(2)
    wvz_in.wait()
    part_rows(wvz, wide, 4, lambda s: 256 + 128 * s, 16)
    for d in (3, 1, 2):
        norm_block(((x + d) % 4) * 2 + c)
    for d in (0, 3, 1, 2):
        slot = ((x + d) % 4) * 2 + 1 - c
        wait_bytes(hall.at[slot], ag_r.at[slot])
        norm_block(slot)

    left = nrm[...].astype(BF16)
    for n in range(3):
        proj[:, 256 * n : 256 * n + 256] = mm(left, wide[:, 256 * n : 256 * n + 256])
    wba = wba_ref[...].astype(F32)
    wba = jnp.concatenate([wba[0], wba[1], jnp.zeros((4, 2048), F32)], axis=0).astype(BF16)
    bas[...] = lax.dot_general(left, wba, (((1,), (1,)), ((), ())), preferred_element_type=F32)

    states_in.wait()
    wo_in.wait()

    def gated_rows(o):
        at = pl.multiple_of(o * 24, 8)
        return delta_rows(
            proj[pl.ds(at, 24)], bas[pl.ds(at, 24)], (alog_ref[...], dt_ref[...]), gain_gate[...],
            states[pl.ds(pl.multiple_of(o * 8, 8), 8)],
        )

    def partial_rows(o):
        gated = jnp.concatenate([gated_rows(o), jnp.zeros((8, 256), F32)], axis=0).astype(BF16)
        return mm(gated, wo[...])[:24].reshape(3, 8, 2048)

    others = [((x + d) % 4) * 2 + 1 - c for d in (2, 1, 3)]
    gated = jnp.concatenate([gated_rows(o) for o in others] + [jnp.zeros((24, 256), F32)], axis=0)
    rows = mm(gated.astype(BF16), wo[...])
    for k, o in enumerate(others):
        partb[o] = rows[24 * k : 24 * k + 24].reshape(3, 8, 2048).astype(BF16)
        remote(partb.at[o], fs.at[k], f_s, f_r.at[k], (b, sib)).start()

    @pl.loop(0, 3)
    def _(k):
        o = ((x + 2 - k + 3 * (k // 2)) % 4) * 2 + c
        rows = partial_rows(o)
        wait_bytes(fs.at[k], f_r.at[k])
        partb[o] = (rows + fs[k].astype(F32)).astype(BF16)
        remote(partb.at[o], rs.at[k], rs_s, rs_r, (b, o)).start()

    partb[sib] = partial_rows(sib).astype(BF16)
    remote(partb.at[sib], rs.at[3], rs_s, rs_r, (b, sib)).start()
    total = partial_rows(h)

    i0, i1 = iota((128, 128), 0), iota((128, 128), 1)
    later = one_hot((i0 // 32 == i1 // 32) & (i1 < i0)).astype(BF16)
    own = jnp.concatenate([ids_ref[...].reshape(24, 10), jnp.full((8, 10), -1, jnp.int32)], axis=0)
    own = jnp.concatenate([own] * 4, axis=0)
    col = iota((128, 256), 1)
    col_chunk, col_rank = (col // 4) % 4, (col % 2).astype(F32)
    named = head_at((col // 16) % 8, 1) * 2 + (col // 2) % 2
    row_chunk = iota((128, 256), 0) // 32

    @pl.loop(0, 8)
    def _(g):
        first, second = batch_at(2 * g, 1) * 16, batch_at(2 * g + 1, 1) * 16
        hot = count_hits(own, named + jnp.where(col < 128, first, second))
        before = mm(later, hot.astype(BF16))
        chosen = jnp.where((before == col_rank) & (row_chunk == col_chunk), hot, 0.0)
        placing[g] = chosen.T.astype(BF16)

    sraw_in.wait()
    part_rows(sraw, swin, 8, gate_up_lane, 4)

    wait_bytes(rs, rs_r)
    for i in range(4):
        total = total + rs[i].astype(F32)
    resid = (hid_ref[...].astype(F32) + total).astype(BF16)
    post = rms_scale(resid.astype(F32), gain_post[...].reshape(1, 1, 2048)).astype(BF16)
    rows = post.astype(F32).reshape(24, 2048)
    blank = jnp.zeros((8, 512), F32)
    stacked[...] = jnp.concatenate(
        [v for j in range(4) for v in (rows[:, 512 * j : 512 * j + 512], blank)], axis=0
    ).astype(BF16)

    for i in range(HEADS):
        psend[i, 0] = resid[:, :, 256 * i : 256 * i + 256]
        psend[i, 1] = post[:, :, 256 * i : 256 * i + 256]
    to_heads(lambda to: psend.at[to], slices, p_s, p_r)
    slices[h] = psend[h]

    for part in range(PARTS):
        @pl.loop(CUTS[part] // 16, CUTS[part + 1] // 16)
        def _(g):
            rows = mm(placing[g], stacked[...]).astype(BF16)
            send[pl.ds(g * 16, 16)] = rows.reshape(16, 16, 512)

        for n in far_first(part):
            if n:
                to = (batch_at(n // 8, 1), head_at(n % 8, 1))
                remote(send.at[n], recv.at[n], d_s, d_r.at[part], to).start()
            else:
                pltpu.make_async_copy(send.at[n], recv.at[n], d_r.at[part]).start()


    def lay_out(n):
        raw_in(n).wait()
        part_rows(raw.at[n % 2], win, 8, gate_up_lane, 16, 0, n * 1024)
        if n < 2:
            raw_in(n + 2).start()

    lay_out(0)
    lay_out(1)
    take(slices, p_r)
    every = slices[:, 1].astype(F32).reshape(192, 256)
    up = mm(every.astype(BF16), swin[...])
    sgate = sgate_ref[...].astype(F32)
    logit = jnp.sum(every[:, :128] * sgate[:1] + every[:, 128:] * sgate[1:], axis=-1, keepdims=True)
    high = logit.astype(BF16).astype(F32)
    zero = jnp.zeros((192, 126), F32)
    sp[...] = (
        jnp.concatenate([up, high, logit - high, zero], axis=1).astype(BF16).reshape(HEADS, 3, 8, 1152)
    )
    to_heads(lambda to: sp.at[to], sp_recv, g_s, g_r)

    lay_out(2)
    lay_out(3)

    take(ids_all, i_r)
    take(wts_all, w_r)
    ids = ids_all[...].reshape(192, 10)
    wts = wts_all[...].reshape(192, 10)
    i0, i1 = iota((192, 192), 0), iota((192, 192), 1)
    later2 = one_hot((i0 // 24 == i1 // 24) & (i1 < i0)).astype(BF16)
    cell = iota((192, 64), 1)
    named2 = head_at((cell // 4) % 8, 1) * 2 + (cell // 2) % 2
    rank2 = (iota((192, 64), 1) % 2).astype(F32)
    widen = one_hot(iota((64, 512), 1) // 8 == iota((64, 512), 0)).astype(BF16)
    col2 = iota((384, 512), 1)
    source_head, member = head_at((col2 // 32) % 8, 1), col2 % 8
    owner = ((source_head // 2 + 4 - member // 2) % 4) * 2 + (source_head + member) % 2
    kept = (iota((384, 512), 0) % 192) // 24 == owner

    @pl.loop(0, 8)
    def _(g):
        near, far = batch_at(2 * g, 1) * 16, batch_at(2 * g + 1, 1) * 16
        here = named2 + jnp.where(cell < 32, near, far)
        hot = jnp.zeros((192, 64), F32)
        heavy = jnp.zeros((192, 64), F32)
        for k in range(10):
            same = ids[:, k : k + 1] == here
            hot = hot + one_hot(same)
            heavy = heavy + jnp.where(same, wts[:, k : k + 1], 0.0)
        before = mm(later2, hot.astype(BF16))
        heavy = jnp.where(before == rank2, heavy, 0.0)
        top = heavy.astype(BF16)
        both = jnp.concatenate([top, (heavy - top.astype(F32)).astype(BF16)], axis=0)
        load[g] = jnp.where(kept, mm(both, widen), 0.0).astype(BF16)

    source, inside = iota((256, 256), 1) // 16, iota((256, 256), 1) % 16
    target = (inside // 4) * 64 + ((inside // 2) % 2) * 32 + (source // 8) * 16 + (inside % 2) * 8 + source % 8
    order = one_hot(iota((256, 256), 0) == target).astype(BF16)
    wout_in.wait()
    for part in range(PARTS):
        start, size = CUTS[part], CUTS[part + 1] - CUTS[part]
        wait_bytes(recv.at[pl.ds(start, size)], d_r.at[part])

        @pl.loop(0, size // 16)
        def _(i):
            got = mm(order, recv[pl.ds(start + i * 16, 16)].reshape(256, 512)).astype(BF16)
            to = pl.multiple_of(i * 32, 32)
            for j in range(4):
                for e in range(2):
                    at = j * 64 + e * 32
                    xs[e, pl.ds(to, 32), 512 * j : 512 * j + 512] = got[at : at + 32]

        @pl.loop(0, 2)
        def _(e):
            for n in range(2):
                lane = slice(256 * n, 256 * n + 256)
                lane2 = slice(512 + 256 * n, 768 + 256 * n)
                gate = mm(xs[e, : 2 * size], win[pl.ds(e * 2048, 2048), lane])
                more = mm(xs[e, : 2 * size], win[pl.ds(e * 2048, 2048), lane2])
                inner[e, : 2 * size, lane] = (silu(gate) * more).astype(BF16)

        for member in (4, 5, 2, 3, 6, 7, 0, 1):
            f = head_at(member, -1)
            lane = pl.ds(pl.multiple_of(f * 256, 256), 256)
            for e in range(2):
                got = mm(inner[e, : 2 * size], wout[e, :, lane]).astype(BF16)
                for i in range(size // 8):
                    back[start + 8 * i + member, 16 * e : 16 * e + 16, :] = got[16 * i : 16 * i + 16]
            for n in far_first(part):
                if n % 8 == member:
                    if n:
                        remote(back.at[n], home.at[n], b_s, b_r.at[part], (batch_at(n // 8, -1), f)).start()
                    else:
                        pltpu.make_async_copy(back.at[n], home.at[n], b_r.at[part]).start()

        if part == 0:
            take(sp_recv, g_r)
            total = sp[h].astype(F32)
            for i in range(1, HEADS):
                total = total + sp_recv[(h + i) % HEADS].astype(F32)
            logit = total[:, :, 1024:1025] + total[:, :, 1025:1026]
            mid = silu(total[:, :, :512]) * total[:, :, 512:1024] * jax.nn.sigmoid(logit)
            mids[h] = mid.astype(BF16)
            to_heads(lambda to: mids.at[h], mids, m_s, m_r)

    down_in.wait()
    take(mids, m_r)
    every = mids[...].astype(F32).reshape(192, 512).astype(BF16)
    shared = mm(every, down[...])
    near = slices[:, 0].astype(F32).reshape(192, 256) + shared
    acc = jnp.zeros((384, 256), F32)
    for part in range(PARTS):
        start, size = CUTS[part], CUTS[part + 1] - CUTS[part]
        wait_bytes(home.at[pl.ds(start, size)], b_r.at[part])
        for g in range(start // 16, (start + size) // 16):
            acc = acc + mm(load[g], home[16 * g : 16 * g + 16].reshape(512, 256))
    acc = acc[:192] + acc[192:]
    out = (near + acc.astype(BF16).astype(F32)).astype(BF16).reshape(HEADS, 3, 8, 256)
    for o in range(HEADS):
        out_ref[:, o] = out[o]
    for copy in sent:
        copy.wait_send()
    take(ids_all, i_s)
    take(wts_all, w_s)
    wait_bytes(fs, f_s)
    wait_bytes(rs, rs_s)
    take(psend, p_s)
    take(send, d_s)
    take(sp, g_s)
    take(mids, m_s)
    take(back, b_s)


def layer(*args):
    dma = pltpu.SemaphoreType.DMA
    return pl.pallas_call(
        layer_kernel,
        name="layer",
        out_shape=jax.ShapeDtypeStruct((3, HEADS, 8, 256), BF16),
        in_specs=[ANY] * 18,
        out_specs=VMEM,
        scratch_shapes=[
            pltpu.VMEM((3, 8, 2048), BF16),
            pltpu.VMEM((3, 8, 10), jnp.int32),
            pltpu.VMEM((3, 8, 10), F32),
            pltpu.VMEM((1, 2048), F32),
            pltpu.VMEM((1, 2), F32),
            pltpu.VMEM((1, 2), F32),
            pltpu.VMEM((1, 128), F32),
            pltpu.VMEM((1, 2048), F32),
            pltpu.VMEM((2, 2, 2048), BF16),
            pltpu.VMEM((2, 128), BF16),
            pltpu.VMEM((HEADS, 3, 8, 2048), BF16),
            pltpu.VMEM((192, 2048), F32),
            pltpu.VMEM((192, 768), F32),
            pltpu.VMEM((192, 8), F32),
            pltpu.VMEM((64, 2, 128, 128), F32),
            pltpu.VMEM((4096, 128), BF16),
            pltpu.VMEM((8192, 128), BF16),
            pltpu.VMEM((2048, 768), BF16),
            pltpu.VMEM((256, 2048), BF16),
            pltpu.VMEM((2048, 128), BF16),
            pltpu.VMEM((256, 1024), BF16),
            pltpu.VMEM((512, 256), BF16),
            pltpu.VMEM((2, 8192, 128), BF16),
            pltpu.VMEM((4096, 1024), BF16),
            pltpu.VMEM((2, 512, 2048), BF16),
            pltpu.VMEM((HEADS, 3, 8, 10), jnp.int32),
            pltpu.VMEM((HEADS, 3, 8, 10), F32),
            pltpu.VMEM((HEADS, 3, 8, 2048), BF16),
            pltpu.VMEM((3, 3, 8, 2048), BF16),
            pltpu.VMEM((4, 3, 8, 2048), BF16),
            pltpu.VMEM((DEVS, 16, 512), BF16),
            pltpu.VMEM((DEVS, 16, 512), BF16),
            pltpu.VMEM((HEADS, 2, 3, 8, 256), BF16),
            pltpu.VMEM((HEADS, 2, 3, 8, 256), BF16),
            pltpu.VMEM((128, 512), BF16),
            pltpu.VMEM((8, 256, 128), BF16),
            pltpu.VMEM((8, 384, 512), BF16),
            pltpu.VMEM((2, 2 * max(b - a for a, b in zip(CUTS, CUTS[1:])), 2048), BF16),
            pltpu.VMEM((2, 2 * max(b - a for a, b in zip(CUTS, CUTS[1:])), 512), BF16),
            pltpu.VMEM((DEVS, 32, 256), BF16),
            pltpu.VMEM((DEVS, 32, 256), BF16),
            pltpu.VMEM((HEADS, 3, 8, 1152), BF16),
            pltpu.VMEM((HEADS, 3, 8, 1152), BF16),
            pltpu.VMEM((HEADS, 3, 8, 512), BF16),
            dma((10,)), dma((7,)), dma((2,)), dma((7,)), dma((HEADS,)),
        ]
        + [dma(())] * 5
        + [dma((3,))]
        + [dma(())] * 5
        + [dma((PARTS,)), dma(()), dma((PARTS,))]
        + [dma(())] * 4,
        compiler_params=pltpu.CompilerParams(
            collective_id=0, has_side_effects=True, vmem_limit_bytes=55 * 2**20
        ),
    )(*args)


def column_rows(w):
    return w.reshape(-1, 2, 4, 128).transpose(0, 2, 1, 3).reshape(-1, 128)


def shards(
    hidden_in, states, norm_in, w_qk, w_vz, w_ba, a_log, dt_bias, norm_gate, w_out, norm_post,
    shared_in, shared_gate, shared_out, expert_in, expert_out, routes, route_weight,
):
    out = layer(
        hidden_in.transpose(1, 0, 2),
        routes.transpose(1, 0, 2),
        route_weight.transpose(1, 0, 2),
        norm_in.reshape(1, 2048),
        a_log.reshape(1, 2),
        dt_bias.reshape(1, 2),
        norm_gate.reshape(1, 128),
        norm_post.reshape(1, 2048),
        w_ba.transpose(1, 2, 0),
        shared_gate.reshape(2, 128),
        states,
        w_qk.reshape(4096, 128),
        w_vz.reshape(8192, 128),
        w_out.reshape(256, 2048),
        column_rows(shared_in),
        shared_out,
        column_rows(expert_in),
        expert_out,
    )
    return out.reshape(3, 64, 256).transpose(1, 0, 2)


def solution(mesh):
    in_specs = (
        P(("batch", "head"), None, None),
        P("batch", "head", None, None),
        P(),
        P(None, "head", None, None),
        P(None, "head", None, None),
        P(None, None, "head"),
        P("head"),
        P("head"),
        P(),
        P("head", None, None),
        P(),
        P("head", None, None),
        P("head"),
        P(None, "head"),
        P(("batch", "head"), None, None, None),
        P(("batch", "head"), None, None),
        P(("batch", "head"), None, None),
        P(("batch", "head"), None, None),
    )
    out_specs = P("batch", None, "head")
    return jax.shard_map(shards, mesh=mesh, in_specs=in_specs, out_specs=out_specs, check_vma=False)
```
